32 devices in a mesh: seq: 16 (over z, y, x), head: 2 (over core).
Axes of the slice: x: 2, y: 2, z: 4, core: 2. Of those that a mesh axis runs over, the one named last changes fastest.
Arguments:
- query_vec: bfloat16 [16384, 2048], P('seq', 'head'), may hold values from -6 to 6
- key_vec: bfloat16 [16384, 2048], P('seq', 'head'), may hold values from -6 to 6
- value_vec: bfloat16 [16384, 2048], P('seq', 'head'), may hold values from -60 to 60
- cotangent: bfloat16 [16384, 2048], P('seq', 'head'), may hold values from -6 to 6
- norm_gain: float32 [2048], P('head'), may hold values from 0.5 to 1.5
- doc_ids: int32 [16384], P('seq'), may hold values from 0 to 15, never falling along the last dimension, each value on 1 to 4096 neighbouring positions
- lang_ids: int32 [16384], P('seq'), may hold values from 0 to 15
- loss_table: float32 [16], replicated, may hold values from 0.25 to 4
Outputs:
- grad_query: bfloat16 [16384, 2048], P('seq', 'head')
- grad_key: bfloat16 [16384, 2048], P('seq', 'head')
- grad_value: bfloat16 [16384, 2048], P('seq', 'head')
The draws below stay inside these ranges and needn't reach their ends.
Inputs may be any that keep to these rules, and one draw needn't show every extreme that they name: `doc_ids`: document numbers never fall along the row, each of 0 to 15 occurs, every document has 1 to 4096 tokens and one has exactly 4096.
All inputs are finite; a program needn't handle non-finite values.
Results may differ from the reference program's by a relative error of at most 0.0058.
Values sent between devices are 32-bit elements; how exact they have to be, the bound alone decides.
A program may use at most 128 MiB of HBM per device.

```python
import math
import jax
import jax.numpy as jnp
import numpy as np
from jax import lax

HEAD_DIM = 128
HEADS = 16
TOK_DEV = 1024
NLANG = 16
TOKENS = 16384
DOCS = 16
DOC_MOST = 4096


def draw_value_vec(key, part):
    key_base, key_rough = jax.random.split(key, 2)
    columns = HEADS * HEAD_DIM
    ramp = jnp.arange(columns, dtype=jnp.float32) / (columns - 1)
    base = jnp.clip(jax.random.normal(key_base, (TOKENS, columns), jnp.float32), -6.0, 6.0)
    slope = math.log(3.0)
    rough = jnp.exp(jax.random.uniform(key_rough, (columns,), jnp.float32, 0.0, math.log(3.3)))
    return (base * jnp.exp(slope * ramp)[None, :] * rough[None, :]).astype(jnp.bfloat16)


def plant(values, rng, low, top_value):
    longest = values.shape.index(max(values.shape))
    spots = []
    for shift in (0, 1):
        where = [jax.random.randint(jax.random.fold_in(rng, axis), (), 0, length) for axis, length in enumerate(values.shape)]
        where[longest] = (where[longest] + shift) % values.shape[longest]
        spots.append(tuple(where))
    return values.at[spots[0]].set(low).at[spots[1]].set(top_value)


def level_of(own_key, extent, pieces, smallest, largest):
    def one(dim, parts):
        steps = jax.random.uniform(jax.random.fold_in(jax.random.fold_in(own_key, 6), dim), (parts,), jnp.float32, smallest / len(pieces), largest / len(pieces))
        return jnp.repeat(jnp.exp(steps), extent[dim] // parts).reshape((-1,) + (1,) * (len(extent) - dim - 1))

    gain = one(*pieces[0])
    for cut in pieces[1:]:
        gain = gain * one(*cut)
    return gain


def profile(amount, total, reach, skew):
    portions = [(1 << 20) // math.isqrt(standing ** skew) + 1 for standing in range(2, amount + 1)]
    rest, holding = total - reach - (amount - 1), [1] * (amount - 1)
    while rest > 0:
        free = [i for i in range(amount - 1) if holding[i] < reach]
        whole, remaining = sum([portions[i] for i in free]), rest
        for i in free:
            addition = min(reach - holding[i], max(1, remaining * portions[i] // whole), rest)
            holding[i] = holding[i] + addition
            rest = rest - addition
    return np.array([reach] + holding)


def ragged(stream_key, amount, total, limit, lean):
    if amount == 2:
        one = jax.random.randint(stream_key, (), max(1, total - limit), min(limit, total - 1) + 1)
        return jnp.stack([one, total - one])
    sizes = jnp.asarray(profile(amount, total, limit, lean), jnp.int32)
    twos = (amount - 1) // 2
    source_of, taker = sizes[1:1 + 2 * twos:2], sizes[2:2 + 2 * twos:2]
    room = jnp.minimum(source_of - 1, limit - taker)
    shifted = jax.random.randint(jax.random.fold_in(stream_key, 1), (twos,), 0, 1 << 20) % (room + 1)
    sizes = sizes.at[1:1 + 2 * twos:2].set(source_of - shifted).at[2:2 + 2 * twos:2].set(taker + shifted)
    return sizes[jax.random.permutation(jax.random.fold_in(stream_key, 2), amount)]


def centred(rng, shape, scale, reach, shards=(), kind=jnp.bfloat16):
    values = jax.random.normal(rng, shape, jnp.float32) * scale
    if len(shards) > 0:
        values = level_of(rng, shape, shards, -0.22, 0.18) * values
    return jnp.clip(values, min=-reach, max=reach).astype(kind)


def setup_inputs(seed: int = 0) -> dict:
    key_list = jax.random.split(jax.random.key(seed), 9)
    return {
        "query_vec": centred(key_list[0], (TOKENS, HEADS * HEAD_DIM), 1.0, 6.0, ((0, 16), (1, 2))),
        "key_vec": centred(key_list[1], (TOKENS, HEADS * HEAD_DIM), 1.0, 6.0, ((0, 16), (1, 2))),
        "value_vec": draw_value_vec(jax.random.fold_in(key_list[8], 71), 0),
        "cotangent": centred(key_list[3], (TOKENS, HEADS * HEAD_DIM), 1.0, 6.0, ((0, 16), (1, 2))),
        "norm_gain": jnp.clip(0.5 + 1.0 * jax.random.uniform(key_list[4], (HEADS * HEAD_DIM,), jnp.float32) ** level_of(key_list[4], (HEADS * HEAD_DIM,), ((0, 2),), -0.2, 0.2), 0.5, 1.5),
        "doc_ids": jnp.searchsorted(jnp.cumsum(ragged(key_list[5], DOCS, TOKENS, DOC_MOST, 2)), jnp.arange(TOKENS), side="right").astype(jnp.int32),
        "lang_ids": plant(jax.random.randint(key_list[6], (TOKENS,), 0, NLANG), jax.random.fold_in(key_list[6], 1), 0, NLANG - 1).astype(jnp.int32),
        "loss_table": jnp.clip(jnp.exp(jax.random.uniform(key_list[7], (NLANG,), jnp.float32, math.log(0.25), math.log(4.0))), 0.25, 4.0),
    }


EPSILON = 1e-06

def rounded(tensor):
    return lax.optimization_barrier(tensor.astype(jnp.bfloat16)).astype(jnp.float32)

def as_float(tensor):
    return tensor.astype(jnp.float32)

def visible_mask(doc_block):
    position = jnp.arange(doc_block.shape[0])
    causal = position[:, None] >= position[None, :]
    return causal & (doc_block[:, None] == doc_block[None, :])

def block_scores(query_blk, key_blk, doc_block):
    raw_scores = jnp.einsum('the,she->hts', as_float(query_blk), as_float(key_blk))
    return rounded(jnp.where(visible_mask(doc_block)[None], raw_scores, 0.0))

def forward_state(inputs):
    key_blk, value_blk, doc_block = inputs
    kept_keys = jnp.where((doc_block == doc_block[-1])[:, None, None], as_float(key_blk), 0.0)
    return jnp.einsum('the,thf->hef', kept_keys, as_float(value_blk))

def backward_state(inputs):
    query_blk, grad_blk, doc_block = inputs
    kept_queries = jnp.where((doc_block == doc_block[0])[:, None, None], as_float(query_blk), 0.0)
    return jnp.einsum('the,thf->hef', kept_queries, as_float(grad_blk))

def head_block(inputs):
    query_blk, key_blk, value_blk, doc_block, incoming_blk = inputs
    scores = block_scores(query_blk, key_blk, doc_block)
    inner = jnp.einsum('hts,shf->thf', scores, as_float(value_blk))
    carried = jnp.einsum('the,hef->thf', as_float(query_blk), incoming_blk)
    in_first = (doc_block == doc_block[0])[:, None, None]
    return inner + jnp.where(in_first, carried, 0.0)

def grad_block(inputs):
    query_blk, key_blk, value_blk, grad_blk, doc_block, incoming_blk, returning_blk = inputs
    query_f = as_float(query_blk)
    key_f = as_float(key_blk)
    value_f = as_float(value_blk)
    grad_f = as_float(grad_blk)
    scores = block_scores(query_blk, key_blk, doc_block)
    grad_raw = jnp.einsum('thf,shf->hts', grad_f, value_f)
    grad_scores = rounded(jnp.where(visible_mask(doc_block)[None], grad_raw, 0.0))
    in_first = (doc_block == doc_block[0])[:, None, None]
    in_last = (doc_block == doc_block[-1])[:, None, None]
    grad_q = jnp.einsum('hts,she->the', grad_scores, key_f) + jnp.where(in_first, jnp.einsum('thf,hef->the', grad_f, incoming_blk), 0.0)
    grad_k = jnp.einsum('hts,the->she', grad_scores, query_f) + jnp.where(in_last, jnp.einsum('shf,hef->she', value_f, returning_blk), 0.0)
    grad_v = jnp.einsum('hts,thf->shf', scores, grad_f) + jnp.where(in_last, jnp.einsum('she,hef->shf', key_f, returning_blk), 0.0)
    return (grad_q.astype(jnp.bfloat16), grad_k.astype(jnp.bfloat16), grad_v.astype(jnp.bfloat16))

def carry_forward(carry, inputs):
    running, prev_last = carry
    state_blk, first_doc, last_doc = inputs
    incoming = jnp.where(prev_last == first_doc, running, 0.0)
    running = state_blk + jnp.where(prev_last == last_doc, running, 0.0)
    return ((running, last_doc), incoming)

def carry_backward(carry, inputs):
    running, next_first = carry
    back_blk, first_doc, last_doc = inputs
    returning = jnp.where(next_first == last_doc, running, 0.0)
    running = back_blk + jnp.where(next_first == first_doc, running, 0.0)
    return ((running, first_doc), returning)

def reference(query_vec, key_vec, value_vec, cotangent, norm_gain, doc_ids, lang_ids, loss_table):
    block_count = TOKENS // TOK_DEV
    norm_width = HEADS * HEAD_DIM

    def split_blocks(tensor):
        return tensor.reshape(block_count, TOK_DEV, HEADS, HEAD_DIM)
    queries = split_blocks(query_vec)
    keys_all = split_blocks(key_vec)
    values_all = split_blocks(value_vec)
    doc_blocks = doc_ids.reshape(block_count, TOK_DEV)
    first_docs = doc_blocks[:, 0]
    last_docs = doc_blocks[:, TOK_DEV - 1]
    states = lax.map(forward_state, (keys_all, values_all, doc_blocks))
    start = (jnp.zeros(states.shape[1:], jnp.float32), jnp.array(-1, jnp.int32))
    unused_carry, incoming = lax.scan(carry_forward, start, (states, first_docs, last_docs))
    incoming = rounded(incoming)
    head_out = lax.map(head_block, (queries, keys_all, values_all, doc_blocks, incoming))
    flat = head_out.reshape(TOKENS, norm_width)
    table_hit = lang_ids[:, None] == jnp.arange(NLANG, dtype=jnp.int32)[None, :]
    token_weight = lax.optimization_barrier(jnp.sum(jnp.where(table_hit, loss_table[None, :], 0.0), axis=1))
    scaled = as_float(cotangent) * token_weight[:, None]
    upstream = scaled * norm_gain[None, :]
    inv_rms = lax.rsqrt(lax.optimization_barrier(jnp.sum(flat * flat, axis=1)) / norm_width + EPSILON)
    mixed = lax.optimization_barrier(jnp.sum(upstream * flat, axis=1))
    grad_out = (inv_rms[:, None] * upstream - flat * (inv_rms ** 3 * mixed / norm_width)[:, None]).astype(jnp.bfloat16)
    grads = split_blocks(grad_out)
    backs = lax.map(backward_state, (queries, grads, doc_blocks))
    start_back = (jnp.zeros(backs.shape[1:], jnp.float32), jnp.array(-1, jnp.int32))
    unused_back, returning = lax.scan(carry_backward, start_back, (backs, first_docs, last_docs), reverse=True)
    returning = rounded(returning)
    grad_q, grad_k, grad_v = lax.map(grad_block, (queries, keys_all, values_all, grads, doc_blocks, incoming, returning))
    return (grad_q.reshape(TOKENS, norm_width), grad_k.reshape(TOKENS, norm_width), grad_v.reshape(TOKENS, norm_width))
```

```python
import functools

import jax
import jax.numpy as jnp
from jax import lax
from jax.experimental import pallas as pl
from jax.experimental.pallas import tpu as pltpu
from jax.sharding import PartitionSpec as P

HEAD_DIM = 128
HEADS = 16
EPSILON = 1e-06
TILE = 256
LAG_Y = 2
LAG_Z = 4
MESH = pl.DeviceIdType.MESH
F32 = jnp.float32
BF16 = jnp.bfloat16


def dot_nn(a, b):
    return lax.dot_general(a, b, (((1,), (0,)), ((), ())), preferred_element_type=F32)


def dot_nt(a, b):
    return lax.dot_general(a, b, (((1,), (1,)), ((), ())), preferred_element_type=F32)


def dot_tn(a, b):
    return lax.dot_general(a, b, (((0,), (0,)), ((), ())), preferred_element_type=F32)


def same(a, b):
    return jnp.where(a == b, 1.0, 0.0)


def kernel(
    blocks, cores, norm_width,
    table_ref, doc_ref, lang_ref, gain_ref, q_hbm, k_hbm, v_hbm, c_hbm,
    dq_hbm, dk_hbm, dv_hbm,
    q_s, k_s, v_s, c_s, g_s, out_s, dv_s, st_s, mask_s, maskt_s,
    own_s, xin_s, pair_s, yin_s, send_s, zin_s, carry_s, inc_s, ret_s,
    col_s, first_s, last_s, sq_s, mx_s, stat_s, statin_s, meta_s,
    in_sem, out_sem, comm_send, comm_recv, meta_send, meta_recv, stat_send, stat_recv,
):
    heads, rows, _ = q_s.shape
    count = rows // TILE
    here = lax.axis_index("seq")
    core = lax.axis_index("head")
    bit_x = lax.rem(here, 2)
    bit_y = lax.rem(here // 2, 2)
    near = here + 1 - 2 * bit_x
    across = here + 2 - 4 * bit_y
    has_up = here + 4 < blocks
    has_down = here >= 4
    up = jnp.where(has_up, here + 4, here - 4)
    down = jnp.where(has_down, here - 4, here + 4)

    def load(which, h):
        src = (k_hbm, v_hbm, q_hbm, c_hbm)[which]
        dst = (k_s, v_s, q_s, c_s)[which]
        at = pl.ds(pl.multiple_of(h * HEAD_DIM, HEAD_DIM), HEAD_DIM)
        return pltpu.make_async_copy(src.at[:, at], dst.at[h], in_sem.at[which, h])

    def store(which, h):
        src = (c_s, q_s, g_s)[which]
        dst = (dq_hbm, dk_hbm, dv_hbm)[which]
        at = pl.ds(pl.multiple_of(h * HEAD_DIM, HEAD_DIM), HEAD_DIM)
        return pltpu.make_async_copy(src.at[h], dst.at[:, at], out_sem.at[which, h])

    for group in ((0, 1), (2, 3)):
        for h in range(heads):
            for which in group:
                load(which, h).start()

    barrier = pltpu.get_barrier_semaphore()

    def greet(device):
        pl.semaphore_signal(barrier, inc=1, device_id=device, device_id_type=MESH)

    greet((near, core))
    greet((across, core))
    for d in range(1, cores):
        greet((here, lax.rem(core + d, cores)))

    @pl.when(has_up)
    def _():
        greet((up, core))

    @pl.when(has_down)
    def _():
        greet((down, core))

    def remote(src, dst, send_sem, recv_sem, device):
        return pltpu.make_async_remote_copy(
            src_ref=src, dst_ref=dst, send_sem=send_sem, recv_sem=recv_sem,
            device_id=device, device_id_type=MESH,
        )

    def state_copy(back, step, h):
        src = (own_s, pair_s, send_s)[step].at[back, h]
        dst = (xin_s, yin_s, zin_s)[step].at[back, h]
        target = (near, across, down if back else up)[step]
        return remote(
            src, dst, comm_send.at[back, step, h], comm_recv.at[back, step, h], (target, core)
        )

    def meta_copy(step):
        target = (near, across, up, down)[step]
        src = meta_s.at[(0, 2, 4, 4)[step]]
        dst = meta_s.at[(1, 3, 5, 6)[step]]
        return remote(src, dst, meta_send.at[step], meta_recv.at[step], (target, core))

    def stat_copy(d):
        return remote(
            stat_s, statin_s.at[d - 1], stat_send.at[d - 1], stat_recv.at[d - 1],
            (here, lax.rem(core + d, cores)),
        )

    def column(row):
        return jnp.transpose(jnp.broadcast_to(row, (HEAD_DIM, rows)))

    doc_row = doc_ref[...].astype(F32)
    col_s[...] = column(doc_row)
    own_first = col_s[0:1, :]
    own_last = col_s[rows - 1 : rows, :]
    first_s[...] = jnp.where(col_s[...] == own_first, 1.0, 0.0).astype(BF16)
    last_s[...] = jnp.where(col_s[...] == own_last, 1.0, 0.0).astype(BF16)
    meta_s[0, 0:1, :] = own_first
    meta_s[0, 1:2, :] = own_last
    meta_s[0, 2:8, :] = jnp.zeros((6, HEAD_DIM), F32)

    total = 1 + 1 + (cores - 1) + has_up.astype(jnp.int32) + has_down.astype(jnp.int32)
    pl.semaphore_wait(barrier, total)
    meta_copy(0).start()

    @pl.loop(0, heads)
    def _(h):
        load(0, h).wait()
        load(1, h).wait()
        own_s[0, h] = dot_tn(k_s[h] * last_s[...], v_s[h])
        state_copy(0, 0, h).start()

    ahead = lax.broadcasted_iota(jnp.int32, (TILE, HEAD_DIM), 0)
    lane = lax.broadcasted_iota(jnp.int32, (TILE, HEAD_DIM), 1)
    for i in range(count):
        col = col_s[i * TILE : (i + 1) * TILE, :]
        for j in range(rows // HEAD_DIM):
            at = j * HEAD_DIM
            equal = col == doc_row[:, at : at + HEAD_DIM]
            if at < (i + 1) * TILE:
                seen = equal
                if at >= i * TILE:
                    seen = seen & (ahead + i * TILE >= lane + at)
                mask_s[i * TILE : (i + 1) * TILE, at : at + HEAD_DIM] = jnp.where(seen, 1.0, 0.0).astype(BF16)
            if at >= i * TILE:
                seen = equal
                if at < (i + 1) * TILE:
                    seen = seen & (ahead + i * TILE <= lane + at)
                maskt_s[i * TILE : (i + 1) * TILE, at : at + HEAD_DIM] = jnp.where(seen, 1.0, 0.0).astype(BF16)

    lang_row = lang_ref[...]
    weight_row = jnp.zeros((1, rows), F32)
    for i in range(table_ref.shape[0]):
        weight_row = jnp.where(lang_row == i, table_ref[i], weight_row)

    meta_copy(0).wait_recv()
    near_first = meta_s[1, 0:1, :]
    near_last = meta_s[1, 1:2, :]
    pair_first = jnp.where(bit_x == 0, own_first, near_first)
    pair_last = jnp.where(bit_x == 0, near_last, own_last)
    meta_s[2, 0:1, :] = pair_first
    meta_s[2, 1:2, :] = pair_last
    meta_s[2, 2:8, :] = jnp.zeros((6, HEAD_DIM), F32)
    meta_copy(1).start()
    sq_s[...] = jnp.zeros_like(sq_s)
    mx_s[...] = jnp.zeros_like(mx_s)
    meta_copy(1).wait_recv()
    other_first = meta_s[3, 0:1, :]
    other_last = meta_s[3, 1:2, :]
    group_first = jnp.where(bit_y == 0, pair_first, other_first)
    group_last = jnp.where(bit_y == 0, other_last, pair_last)
    meta_s[4, 0:1, :] = group_first
    meta_s[4, 1:2, :] = group_last
    meta_s[4, 2:8, :] = jnp.zeros((6, HEAD_DIM), F32)

    @pl.when(has_up)
    def _():
        meta_copy(2).start()

    @pl.when(has_down)
    def _():
        meta_copy(3).start()

    def factors(x, y, mine, target, theirs, other, group):
        x_on = x.astype(F32)
        y_on = y.astype(F32)
        equal = same(mine, theirs)
        pair = (jnp.where(x == 1, 1.0, equal), jnp.where(x == 1, equal, 1.0))
        take = (x_on * same(theirs, target), y_on * same(other, target))
        send = (same(mine, group), (1.0 - x_on) * same(theirs, group), 1.0 - y_on)
        return pair, take, send

    ahead_w = factors(bit_x, bit_y, own_last, own_first, near_last, other_last, group_last)
    back_w = factors(1 - bit_x, 1 - bit_y, own_first, own_last, near_first, other_first, group_first)

    def step_x(back, h):
        pair = (back_w if back else ahead_w)[0]
        state_copy(back, 0, h).wait_recv()
        pair_s[back, h] = pair[0] * own_s[back, h] + pair[1] * xin_s[back, h]
        state_copy(back, 1, h).start()

    def step_y(back, h):
        take, send = (back_w if back else ahead_w)[1:]
        state_copy(back, 1, h).wait_recv()
        near_state = xin_s[back, h]
        far_state = yin_s[back, h]
        send_s[back, h] = send[0] * own_s[back, h] + send[1] * near_state + send[2] * far_state

        @pl.when(has_down if back else has_up)
        def _():
            state_copy(back, 2, h).start()

        carry_s[back, h] = take[0] * near_state + take[1] * far_state

    def step_z(back, h):
        target = own_last if back else own_first

        @pl.when(has_up if back else has_down)
        def _():
            if back:
                end = meta_s[6, 0:1, :]
            else:
                end = meta_s[5, 1:2, :]
            state_copy(back, 2, h).wait_recv()
            carry_s[back, h] += same(end, target) * zin_s[back, h]

        return carry_s[back, h].astype(BF16)

    @pl.when(has_down)
    def _():
        meta_copy(2).wait_recv()

    @pl.when(has_up)
    def _():
        meta_copy(3).wait_recv()

    @pl.loop(0, heads + LAG_Z)
    def _(t):
        @pl.when(t < heads)
        def _():
            load(2, t).wait()
            load(3, t).wait()
            for i in range(count):
                lo, hi = i * TILE, (i + 1) * TILE
                scores = dot_nt(q_s[t, lo:hi, :], k_s[t, :hi, :]).astype(BF16) * mask_s[lo:hi, :hi]
                out_s[t, lo:hi, :] = dot_nn(scores, v_s[t, :hi, :])
                turned = dot_nt(k_s[t, lo:hi, :], q_s[t, lo:, :]).astype(BF16)
                st_s[t, lo:hi, lo:] = turned * maskt_s[lo:hi, lo:]
            step_x(0, t)

        @pl.when((t >= LAG_Y) & (t < heads + LAG_Y))
        def _():
            step_y(0, t - LAG_Y)

        @pl.when(t >= LAG_Z)
        def _():
            h = t - LAG_Z
            incoming = step_z(0, h)
            inc_s[h] = incoming
            out = out_s[h] + dot_nn(q_s[h] * first_s[...], incoming)
            out_s[h] = out
            sq_s[...] += out * out
            gain = gain_ref[:, pl.ds(pl.multiple_of(h * HEAD_DIM, HEAD_DIM), HEAD_DIM)]
            mx_s[...] += c_s[h].astype(F32) * gain * out

    stat_s[0:1, :] = jnp.sum(jnp.transpose(sq_s[...]), axis=0, keepdims=True)
    stat_s[1:2, :] = jnp.sum(jnp.transpose(mx_s[...]), axis=0, keepdims=True)
    stat_s[2:8, :] = jnp.zeros((6, rows), F32)
    for d in range(1, cores):
        stat_copy(d).start()
    squares = stat_s[0:1, :]
    mixed = stat_s[1:2, :]
    for d in range(1, cores):
        stat_copy(d).wait_recv()
        squares = squares + statin_s[d - 1, 0:1, :]
        mixed = mixed + statin_s[d - 1, 1:2, :]
    inv_rms = lax.rsqrt(squares / norm_width + EPSILON)
    sq_s[...] = column(inv_rms * weight_row)
    mx_s[...] = column(inv_rms * inv_rms * inv_rms * (mixed * weight_row) / norm_width)

    @pl.loop(0, heads)
    def _(h):
        gain = gain_ref[:, pl.ds(pl.multiple_of(h * HEAD_DIM, HEAD_DIM), HEAD_DIM)]
        grad = c_s[h].astype(F32) * gain * sq_s[...] - out_s[h] * mx_s[...]
        grad = grad.astype(BF16)
        g_s[h] = grad
        own_s[1, h] = dot_tn(q_s[h] * first_s[...], grad)
        state_copy(1, 0, h).start()

    @pl.loop(0, heads + LAG_Z)
    def _(t):
        @pl.when(t < heads)
        def _():
            for i in range(count):
                lo, hi = i * TILE, (i + 1) * TILE
                scores = dot_nt(g_s[t, lo:hi, :], v_s[t, :hi, :]).astype(BF16) * mask_s[lo:hi, :hi]
                grad_q = dot_nn(scores, k_s[t, :hi, :])
                grad_q += dot_nt(g_s[t, lo:hi, :] * first_s[lo:hi, :], inc_s[t])
                c_s[t, lo:hi, :] = grad_q.astype(BF16)
                turned = dot_nt(v_s[t, lo:hi, :], g_s[t, lo:, :]).astype(BF16) * maskt_s[lo:hi, lo:]
                out_s[t, lo:hi, :] = dot_nn(turned, q_s[t, lo:, :])
                dv_s[t, lo:hi, :] = dot_nn(st_s[t, lo:hi, lo:], g_s[t, lo:, :])
            store(0, t).start()
            step_x(1, t)

        @pl.when((t >= LAG_Y) & (t < heads + LAG_Y))
        def _():
            step_y(1, t - LAG_Y)

        @pl.when(t >= LAG_Z)
        def _():
            h = t - LAG_Z
            returning = step_z(1, h)
            ret_s[...] = returning
            q_s[h] = (out_s[h] + dot_nt(v_s[h] * last_s[...], ret_s[...])).astype(BF16)
            store(1, h).start()
            g_s[h] = (dv_s[h] + dot_nn(k_s[h] * last_s[...], ret_s[...])).astype(BF16)
            store(2, h).start()

    @pl.loop(0, heads)
    def _(h):
        for which in range(3):
            store(which, h).wait()
        for back in range(2):
            state_copy(back, 0, h).wait_send()
            state_copy(back, 1, h).wait_send()

            @pl.when(has_down if back else has_up)
            def _():
                state_copy(back, 2, h).wait_send()

    meta_copy(0).wait_send()
    meta_copy(1).wait_send()

    @pl.when(has_up)
    def _():
        meta_copy(2).wait_send()

    @pl.when(has_down)
    def _():
        meta_copy(3).wait_send()

    for d in range(1, cores):
        stat_copy(d).wait_send()


def local(blocks, cores, query_vec, key_vec, value_vec, cotangent, norm_gain, doc_ids, lang_ids, loss_table):
    rows, cols = query_vec.shape
    heads = cols // HEAD_DIM
    state = (2, heads, HEAD_DIM, HEAD_DIM)
    per_head = (heads, rows, HEAD_DIM)
    any_spec = pl.BlockSpec(memory_space=pl.ANY)
    vmem_spec = pl.BlockSpec(memory_space=pltpu.VMEM)
    shape = jax.ShapeDtypeStruct((rows, cols), BF16)
    return pl.pallas_call(
        functools.partial(kernel, blocks, cores, HEADS * HEAD_DIM),
        out_shape=(shape, shape, shape),
        in_specs=[pl.BlockSpec(memory_space=pltpu.SMEM)] + [vmem_spec] * 3 + [any_spec] * 4,
        out_specs=(any_spec,) * 3,
        scratch_shapes=[pltpu.VMEM(per_head, BF16)] * 5
        + [pltpu.VMEM(per_head, F32)] * 2
        + [pltpu.VMEM((heads, rows, rows), BF16)]
        + [pltpu.VMEM((rows, rows), BF16)] * 2
        + [pltpu.VMEM(state, F32)] * 7
        + [
            pltpu.VMEM(state[1:], BF16),
            pltpu.VMEM(state[2:], BF16),
            pltpu.VMEM((rows, HEAD_DIM), F32),
            pltpu.VMEM((rows, HEAD_DIM), BF16),
            pltpu.VMEM((rows, HEAD_DIM), BF16),
            pltpu.VMEM((rows, HEAD_DIM), F32),
            pltpu.VMEM((rows, HEAD_DIM), F32),
            pltpu.VMEM((8, rows), F32),
            pltpu.VMEM((max(cores - 1, 1), 8, rows), F32),
            pltpu.VMEM((7, 8, HEAD_DIM), F32),
            pltpu.SemaphoreType.DMA((4, heads)),
            pltpu.SemaphoreType.DMA((3, heads)),
            pltpu.SemaphoreType.DMA((2, 3, heads)),
            pltpu.SemaphoreType.DMA((2, 3, heads)),
            pltpu.SemaphoreType.DMA((4,)),
            pltpu.SemaphoreType.DMA((4,)),
            pltpu.SemaphoreType.DMA((max(cores - 1, 1),)),
            pltpu.SemaphoreType.DMA((max(cores - 1, 1),)),
        ],
        compiler_params=pltpu.CompilerParams(
            collective_id=0, has_side_effects=True, vmem_limit_bytes=58 * 2**20
        ),
    )(
        loss_table,
        doc_ids.reshape(1, rows),
        lang_ids.reshape(1, rows),
        norm_gain.reshape(1, cols),
        query_vec,
        key_vec,
        value_vec,
        cotangent,
    )


def solution(mesh):
    sizes = dict(mesh.shape)
    in_specs = (
        P("seq", "head"),
        P("seq", "head"),
        P("seq", "head"),
        P("seq", "head"),
        P("head"),
        P("seq"),
        P("seq"),
        P(),
    )
    out_specs = (P("seq", "head"), P("seq", "head"), P("seq", "head"))
    body = functools.partial(local, sizes["seq"], sizes["head"])
    return jax.shard_map(body, mesh=mesh, in_specs=in_specs, out_specs=out_specs, check_vma=False)
```

```python
import functools

import jax
import jax.numpy as jnp
from jax import lax
from jax.experimental import pallas as pl
from jax.experimental.pallas import tpu as pltpu
from jax.sharding import PartitionSpec as P

HEAD_DIM = 128
HEADS = 16
EPSILON = 1e-06
TILE = 256
LAG_Y = 2
LAG_Z = 4
VMEM_BYTES = 44 * 2**20
MESH = pl.DeviceIdType.MESH
F32 = jnp.float32
BF16 = jnp.bfloat16


def dot_nn(a, b):
    return lax.dot_general(a, b, (((1,), (0,)), ((), ())), preferred_element_type=F32)


def dot_nt(a, b):
    return lax.dot_general(a, b, (((1,), (1,)), ((), ())), preferred_element_type=F32)


def dot_tn(a, b):
    return lax.dot_general(a, b, (((0,), (0,)), ((), ())), preferred_element_type=F32)


def same(a, b):
    return jnp.where(a == b, 1.0, 0.0)


def kernel(
    blocks, cores, norm_width,
    table_ref, doc_ref, lang_ref, gain_ref, q_hbm, k_hbm, v_hbm, c_hbm,
    dq_hbm, dk_hbm, dv_hbm,
    q_s, k_s, v_s, c_s, g_s, out_s, dv_s, st_s, mask_s, maskt_s,
    own_s, xin_s, pair_s, yin_s, send_s, zin_s, carry_s, inc_s, enter_s,
    col_s, first_s, last_s, sq_s, mx_s, stat_s, statin_s, meta_s,
    in_sem, out_sem, comm_send, comm_recv, meta_send, meta_recv, stat_send, stat_recv,
):
    heads, rows, _ = q_s.shape
    count = rows // TILE
    here = lax.axis_index("seq")
    core = lax.axis_index("head")
    bit_x = lax.rem(here, 2)
    bit_y = lax.rem(here // 2, 2)
    near = here + 1 - 2 * bit_x
    across = here + 2 - 4 * bit_y
    has_up = here + 4 < blocks
    has_down = here >= 4
    up = jnp.where(has_up, here + 4, here - 4)
    down = jnp.where(has_down, here - 4, here + 4)

    def load(which, h):
        src = (k_hbm, v_hbm, q_hbm, c_hbm)[which]
        dst = (k_s, v_s, q_s, c_s)[which]
        at = pl.ds(pl.multiple_of(h * HEAD_DIM, HEAD_DIM), HEAD_DIM)
        return pltpu.make_async_copy(src.at[:, at], dst.at[h], in_sem.at[which, h])

    def store(which, h):
        src = (c_s, q_s, g_s)[which]
        dst = (dq_hbm, dk_hbm, dv_hbm)[which]
        at = pl.ds(pl.multiple_of(h * HEAD_DIM, HEAD_DIM), HEAD_DIM)
        return pltpu.make_async_copy(src.at[h], dst.at[:, at], out_sem.at[which, h])

    for group in ((0, 1), (2, 3)):
        for h in range(heads):
            for which in group:
                load(which, h).start()

    barrier = pltpu.get_barrier_semaphore()

    def greet(device):
        pl.semaphore_signal(barrier, inc=1, device_id=device, device_id_type=MESH)

    greet((near, core))
    greet((across, core))
    for d in range(1, cores):
        greet((here, lax.rem(core + d, cores)))

    @pl.when(has_up)
    def _():
        greet((up, core))

    @pl.when(has_down)
    def _():
        greet((down, core))

    def remote(src, dst, send_sem, recv_sem, device):
        return pltpu.make_async_remote_copy(
            src_ref=src, dst_ref=dst, send_sem=send_sem, recv_sem=recv_sem,
            device_id=device, device_id_type=MESH,
        )

    def state_copy(back, step, h):
        src = (own_s, pair_s, send_s)[step].at[back, h]
        dst = (xin_s, yin_s, zin_s)[step].at[back, h]
        target = (near, across, down if back else up)[step]
        return remote(
            src, dst, comm_send.at[back, step, h], comm_recv.at[back, step, h], (target, core)
        )

    def meta_copy(step):
        target = (near, across, up, down)[step]
        src = meta_s.at[(0, 2, 4, 4)[step]]
        dst = meta_s.at[(1, 3, 5, 6)[step]]
        return remote(src, dst, meta_send.at[step], meta_recv.at[step], (target, core))

    def stat_copy(d):
        return remote(
            stat_s, statin_s.at[d - 1], stat_send.at[d - 1], stat_recv.at[d - 1],
            (here, lax.rem(core + d, cores)),
        )

    def column(row):
        return jnp.transpose(jnp.broadcast_to(row, (HEAD_DIM, rows)))

    doc_row = doc_ref[...].astype(F32)
    col_s[...] = column(doc_row)
    own_first = col_s[0:1, :]
    own_last = col_s[rows - 1 : rows, :]
    spans = [slice(i * TILE, (i + 1) * TILE) for i in range(count)]
    firsts = [col_s[i * TILE : i * TILE + 1, :] for i in range(count)]
    lasts = [col_s[(i + 1) * TILE - 1 : (i + 1) * TILE, :] for i in range(count)]
    for i, span in enumerate(spans):
        first_s[span, :] = same(col_s[span, :], firsts[i]).astype(BF16)
        last_s[span, :] = same(col_s[span, :], lasts[i]).astype(BF16)
    meta_s[0, 0:1, :] = own_first
    meta_s[0, 1:2, :] = own_last
    meta_s[0, 2:8, :] = jnp.zeros((6, HEAD_DIM), F32)

    total = 1 + 1 + (cores - 1) + has_up.astype(jnp.int32) + has_down.astype(jnp.int32)
    pl.semaphore_wait(barrier, total)
    meta_copy(0).start()

    @pl.loop(0, heads)
    def _(h):
        load(0, h).wait()
        load(1, h).wait()
        running = None
        for i, span in enumerate(spans):
            state = dot_tn(k_s[h, span, :] * last_s[span, :], v_s[h, span, :])
            if i > 0:
                enter_s[0, h, i] = same(lasts[i - 1], firsts[i]) * running
                state = state + same(lasts[i - 1], lasts[i]) * running
            running = state
        own_s[0, h] = running
        state_copy(0, 0, h).start()

    ahead = lax.broadcasted_iota(jnp.int32, (TILE, HEAD_DIM), 0)
    lane = lax.broadcasted_iota(jnp.int32, (TILE, HEAD_DIM), 1)
    for i, span in enumerate(spans):
        col = col_s[span, :]
        for at in range(0, TILE, HEAD_DIM):
            start = i * TILE + at
            equal = col == doc_row[:, start : start + HEAD_DIM]
            mask_s[span, at : at + HEAD_DIM] = jnp.where(equal & (ahead >= lane + at), 1.0, 0.0).astype(BF16)
            maskt_s[span, at : at + HEAD_DIM] = jnp.where(equal & (ahead <= lane + at), 1.0, 0.0).astype(BF16)

    lang_row = lang_ref[...]
    weight_row = jnp.zeros((1, rows), F32)
    for i in range(table_ref.shape[0]):
        weight_row = jnp.where(lang_row == i, table_ref[i], weight_row)

    meta_copy(0).wait_recv()
    near_first = meta_s[1, 0:1, :]
    near_last = meta_s[1, 1:2, :]
    pair_first = jnp.where(bit_x == 0, own_first, near_first)
    pair_last = jnp.where(bit_x == 0, near_last, own_last)
    meta_s[2, 0:1, :] = pair_first
    meta_s[2, 1:2, :] = pair_last
    meta_s[2, 2:8, :] = jnp.zeros((6, HEAD_DIM), F32)
    meta_copy(1).start()
    sq_s[...] = jnp.zeros_like(sq_s)
    mx_s[...] = jnp.zeros_like(mx_s)
    meta_copy(1).wait_recv()
    other_first = meta_s[3, 0:1, :]
    other_last = meta_s[3, 1:2, :]
    group_first = jnp.where(bit_y == 0, pair_first, other_first)
    group_last = jnp.where(bit_y == 0, other_last, pair_last)
    meta_s[4, 0:1, :] = group_first
    meta_s[4, 1:2, :] = group_last
    meta_s[4, 2:8, :] = jnp.zeros((6, HEAD_DIM), F32)

    @pl.when(has_up)
    def _():
        meta_copy(2).start()

    @pl.when(has_down)
    def _():
        meta_copy(3).start()

    def factors(x, y, mine, target, theirs, other, group):
        x_on = x.astype(F32)
        y_on = y.astype(F32)
        equal = same(mine, theirs)
        pair = (jnp.where(x == 1, 1.0, equal), jnp.where(x == 1, equal, 1.0))
        take = (x_on * same(theirs, target), y_on * same(other, target))
        send = (same(mine, group), (1.0 - x_on) * same(theirs, group), 1.0 - y_on)
        return pair, take, send

    ahead_w = factors(bit_x, bit_y, own_last, own_first, near_last, other_last, group_last)
    back_w = factors(1 - bit_x, 1 - bit_y, own_first, own_last, near_first, other_first, group_first)

    def step_x(back, h):
        pair = (back_w if back else ahead_w)[0]
        state_copy(back, 0, h).wait_recv()
        pair_s[back, h] = pair[0] * own_s[back, h] + pair[1] * xin_s[back, h]
        state_copy(back, 1, h).start()

    def step_y(back, h):
        take, send = (back_w if back else ahead_w)[1:]
        state_copy(back, 1, h).wait_recv()
        near_state = xin_s[back, h]
        far_state = yin_s[back, h]
        send_s[back, h] = send[0] * own_s[back, h] + send[1] * near_state + send[2] * far_state

        @pl.when(has_down if back else has_up)
        def _():
            state_copy(back, 2, h).start()

        carry_s[back, h] = take[0] * near_state + take[1] * far_state

    def step_z(back, h):
        target = own_last if back else own_first

        @pl.when(has_up if back else has_down)
        def _():
            if back:
                end = meta_s[6, 0:1, :]
            else:
                end = meta_s[5, 1:2, :]
            state_copy(back, 2, h).wait_recv()
            carry_s[back, h] += same(end, target) * zin_s[back, h]

        return carry_s[back, h]

    @pl.when(has_down)
    def _():
        meta_copy(2).wait_recv()

    @pl.when(has_up)
    def _():
        meta_copy(3).wait_recv()

    @pl.loop(0, heads + LAG_Z)
    def _(t):
        @pl.when(t < heads)
        def _():
            load(2, t).wait()
            load(3, t).wait()
            for span in spans:
                scores = dot_nt(q_s[t, span, :], k_s[t, span, :]).astype(BF16) * mask_s[span, :]
                out_s[t, span, :] = dot_nn(scores, v_s[t, span, :])
                turned = dot_nt(k_s[t, span, :], q_s[t, span, :]).astype(BF16)
                st_s[t, span, :] = turned * maskt_s[span, :]
            step_x(0, t)

        @pl.when((t >= LAG_Y) & (t < heads + LAG_Y))
        def _():
            step_y(0, t - LAG_Y)

        @pl.when(t >= LAG_Z)
        def _():
            h = t - LAG_Z
            incoming = step_z(0, h)
            gain = gain_ref[:, pl.ds(pl.multiple_of(h * HEAD_DIM, HEAD_DIM), HEAD_DIM)]
            for i, span in enumerate(spans):
                state = incoming
                if i > 0:
                    state = enter_s[0, h, i] + same(firsts[i], own_first) * incoming
                state = state.astype(BF16)
                inc_s[h, i] = state
                out = out_s[h, span, :] + dot_nn(q_s[h, span, :] * first_s[span, :], state)
                out_s[h, span, :] = out
                sq_s[span, :] += out * out
                mx_s[span, :] += c_s[h, span, :].astype(F32) * gain * out

    stat_s[0:1, :] = jnp.sum(jnp.transpose(sq_s[...]), axis=0, keepdims=True)
    stat_s[1:2, :] = jnp.sum(jnp.transpose(mx_s[...]), axis=0, keepdims=True)
    stat_s[2:8, :] = jnp.zeros((6, rows), F32)
    for d in range(1, cores):
        stat_copy(d).start()
    squares = stat_s[0:1, :]
    mixed = stat_s[1:2, :]
    for d in range(1, cores):
        stat_copy(d).wait_recv()
        squares = squares + statin_s[d - 1, 0:1, :]
        mixed = mixed + statin_s[d - 1, 1:2, :]
    inv_rms = lax.rsqrt(squares / norm_width + EPSILON)
    sq_s[...] = column(inv_rms * weight_row)
    mx_s[...] = column(inv_rms * inv_rms * inv_rms * (mixed * weight_row) / norm_width)

    @pl.loop(0, heads)
    def _(h):
        gain = gain_ref[:, pl.ds(pl.multiple_of(h * HEAD_DIM, HEAD_DIM), HEAD_DIM)]
        running = None
        for i in reversed(range(count)):
            span = spans[i]
            grad = c_s[h, span, :].astype(F32) * gain * sq_s[span, :] - out_s[h, span, :] * mx_s[span, :]
            grad = grad.astype(BF16)
            g_s[h, span, :] = grad
            state = dot_tn(q_s[h, span, :] * first_s[span, :], grad)
            if i < count - 1:
                enter_s[1, h, i] = same(firsts[i + 1], lasts[i]) * running
                state = state + same(firsts[i + 1], firsts[i]) * running
            running = state
        own_s[1, h] = running
        state_copy(1, 0, h).start()

    @pl.loop(0, heads + LAG_Z)
    def _(t):
        @pl.when(t < heads)
        def _():
            for i, span in enumerate(spans):
                scores = dot_nt(g_s[t, span, :], v_s[t, span, :]).astype(BF16) * mask_s[span, :]
                grad_q = dot_nn(scores, k_s[t, span, :])
                grad_q += dot_nt(g_s[t, span, :] * first_s[span, :], inc_s[t, i])
                c_s[t, span, :] = grad_q.astype(BF16)
                turned = dot_nt(v_s[t, span, :], g_s[t, span, :]).astype(BF16) * maskt_s[span, :]
                out_s[t, span, :] = dot_nn(turned, q_s[t, span, :])
                dv_s[t, span, :] = dot_nn(st_s[t, span, :], g_s[t, span, :])
            store(0, t).start()
            step_x(1, t)

        @pl.when((t >= LAG_Y) & (t < heads + LAG_Y))
        def _():
            step_y(1, t - LAG_Y)

        @pl.when(t >= LAG_Z)
        def _():
            h = t - LAG_Z
            returning = step_z(1, h)
            for i, span in enumerate(spans):
                state = returning
                if i < count - 1:
                    state = enter_s[1, h, i] + same(lasts[i], own_last) * returning
                state = state.astype(BF16)
                grad_k = out_s[h, span, :] + dot_nt(v_s[h, span, :] * last_s[span, :], state)
                q_s[h, span, :] = grad_k.astype(BF16)
                grad_v = dv_s[h, span, :] + dot_nn(k_s[h, span, :] * last_s[span, :], state)
                g_s[h, span, :] = grad_v.astype(BF16)
            store(1, h).start()
            store(2, h).start()

    @pl.loop(0, heads)
    def _(h):
        for which in range(3):
            store(which, h).wait()
        for back in range(2):
            state_copy(back, 0, h).wait_send()
            state_copy(back, 1, h).wait_send()

            @pl.when(has_down if back else has_up)
            def _():
                state_copy(back, 2, h).wait_send()

    meta_copy(0).wait_send()
    meta_copy(1).wait_send()

    @pl.when(has_up)
    def _():
        meta_copy(2).wait_send()

    @pl.when(has_down)
    def _():
        meta_copy(3).wait_send()

    for d in range(1, cores):
        stat_copy(d).wait_send()


def local(blocks, cores, query_vec, key_vec, value_vec, cotangent, norm_gain, doc_ids, lang_ids, loss_table):
    rows, cols = query_vec.shape
    heads = cols // HEAD_DIM
    count = rows // TILE
    state = (2, heads, HEAD_DIM, HEAD_DIM)
    per_head = (heads, rows, HEAD_DIM)
    any_spec = pl.BlockSpec(memory_space=pl.ANY)
    hbm_spec = pl.BlockSpec(memory_space=pltpu.HBM)
    vmem_spec = pl.BlockSpec(memory_space=pltpu.VMEM)
    shape = jax.ShapeDtypeStruct((rows, cols), BF16)
    return pl.pallas_call(
        functools.partial(kernel, blocks, cores, HEADS * HEAD_DIM),
        out_shape=(shape, shape, shape),
        in_specs=[pl.BlockSpec(memory_space=pltpu.SMEM)] + [vmem_spec] * 3 + [hbm_spec] * 4,
        out_specs=(any_spec,) * 3,
        scratch_shapes=[pltpu.VMEM(per_head, BF16)] * 5
        + [pltpu.VMEM(per_head, F32)] * 2
        + [pltpu.VMEM((heads, rows, TILE), BF16)]
        + [pltpu.VMEM((rows, TILE), BF16)] * 2
        + [pltpu.VMEM(state, F32)] * 7
        + [
            pltpu.VMEM((heads, count) + state[2:], BF16),
            pltpu.VMEM((2, heads, count) + state[2:], F32),
            pltpu.VMEM((rows, HEAD_DIM), F32),
            pltpu.VMEM((rows, HEAD_DIM), BF16),
            pltpu.VMEM((rows, HEAD_DIM), BF16),
            pltpu.VMEM((rows, HEAD_DIM), F32),
            pltpu.VMEM((rows, HEAD_DIM), F32),
            pltpu.VMEM((8, rows), F32),
            pltpu.VMEM((max(cores - 1, 1), 8, rows), F32),
            pltpu.VMEM((7, 8, HEAD_DIM), F32),
            pltpu.SemaphoreType.DMA((4, heads)),
            pltpu.SemaphoreType.DMA((3, heads)),
            pltpu.SemaphoreType.DMA((2, 3, heads)),
            pltpu.SemaphoreType.DMA((2, 3, heads)),
            pltpu.SemaphoreType.DMA((4,)),
            pltpu.SemaphoreType.DMA((4,)),
            pltpu.SemaphoreType.DMA((max(cores - 1, 1),)),
            pltpu.SemaphoreType.DMA((max(cores - 1, 1),)),
        ],
        compiler_params=pltpu.CompilerParams(
            collective_id=0, has_side_effects=True, vmem_limit_bytes=VMEM_BYTES
        ),
    )(
        loss_table,
        doc_ids.reshape(1, rows),
        lang_ids.reshape(1, rows),
        norm_gain.reshape(1, cols),
        query_vec,
        key_vec,
        value_vec,
        cotangent,
    )


def solution(mesh):
    sizes = dict(mesh.shape)
    in_specs = (
        P("seq", "head"),
        P("seq", "head"),
        P("seq", "head"),
        P("seq", "head"),
        P("head"),
        P("seq"),
        P("seq"),
        P(),
    )
    out_specs = (P("seq", "head"), P("seq", "head"), P("seq", "head"))
    body = functools.partial(local, sizes["seq"], sizes["head"])
    return jax.shard_map(body, mesh=mesh, in_specs=in_specs, out_specs=out_specs, check_vma=False)
```

```python
import functools

import jax
import jax.numpy as jnp
from jax import lax
from jax.experimental import pallas as pl
from jax.experimental.pallas import tpu as pltpu
from jax.sharding import PartitionSpec as P

HEAD_DIM = 128
HEADS = 16
EPSILON = 1e-06
TILE = 256
LAG_Y = 2
LAG_Z = 4
VMEM_BYTES = 44 * 2**20
MESH = pl.DeviceIdType.MESH
F32 = jnp.float32
BF16 = jnp.bfloat16


def dot_nn(a, b):
    return lax.dot_general(a, b, (((1,), (0,)), ((), ())), preferred_element_type=F32)


def dot_nt(a, b):
    return lax.dot_general(a, b, (((1,), (1,)), ((), ())), preferred_element_type=F32)


def dot_tn(a, b):
    return lax.dot_general(a, b, (((0,), (0,)), ((), ())), preferred_element_type=F32)


def same(a, b):
    return jnp.where(a == b, 1.0, 0.0)


def kernel(
    blocks, cores, norm_width,
    table_ref, doc_ref, lang_ref, gain_ref, q_hbm, k_hbm, v_hbm, c_hbm,
    dq_ref, dk_ref, dv_ref,
    q_s, k_s, v_s, c_s, g_s, out_s, part_s, dv_s, st_s, mask_s, maskt_s,
    own_s, xin_s, pair_s, yin_s, send_s, zin_s, carry_s, inc_s, enter_s,
    col_s, first_s, last_s, sq_s, mx_s, stat_s, statin_s, meta_s,
    in_sem, comm_send, comm_recv, meta_send, meta_recv, stat_send, stat_recv,
):
    heads, rows, _ = q_s.shape
    count = rows // TILE
    here = lax.axis_index("seq")
    core = lax.axis_index("head")
    bit_x = lax.rem(here, 2)
    bit_y = lax.rem(here // 2, 2)
    near = here + 1 - 2 * bit_x
    across = here + 2 - 4 * bit_y
    has_up = here + 4 < blocks
    has_down = here >= 4
    up = jnp.where(has_up, here + 4, here - 4)
    down = jnp.where(has_down, here - 4, here + 4)

    def load(which, h):
        src = (k_hbm, v_hbm, q_hbm, c_hbm)[which]
        dst = (k_s, v_s, q_s, c_s)[which]
        at = pl.ds(pl.multiple_of(h * HEAD_DIM, HEAD_DIM), HEAD_DIM)
        return pltpu.make_async_copy(src.at[:, at], dst.at[h], in_sem.at[which, h])

    def lanes(h):
        return pl.ds(pl.multiple_of(h * HEAD_DIM, HEAD_DIM), HEAD_DIM)

    for group in ((0, 1), (2, 3)):
        for h in range(heads):
            for which in group:
                load(which, h).start()

    barrier = pltpu.get_barrier_semaphore()

    def greet(device):
        pl.semaphore_signal(barrier, inc=1, device_id=device, device_id_type=MESH)

    greet((near, core))
    greet((across, core))
    for d in range(1, cores):
        greet((here, lax.rem(core + d, cores)))

    @pl.when(has_up)
    def _():
        greet((up, core))

    @pl.when(has_down)
    def _():
        greet((down, core))

    def remote(src, dst, send_sem, recv_sem, device):
        return pltpu.make_async_remote_copy(
            src_ref=src, dst_ref=dst, send_sem=send_sem, recv_sem=recv_sem,
            device_id=device, device_id_type=MESH,
        )

    def state_copy(back, step, h):
        src = (own_s, pair_s, send_s)[step].at[back, h]
        dst = (xin_s, yin_s, zin_s)[step].at[back, h]
        target = (near, across, down if back else up)[step]
        return remote(
            src, dst, comm_send.at[back, step, h], comm_recv.at[back, step, h], (target, core)
        )

    def meta_copy(step):
        target = (near, across, up, down)[step]
        src = meta_s.at[(0, 2, 4, 4)[step]]
        dst = meta_s.at[(1, 3, 5, 6)[step]]
        return remote(src, dst, meta_send.at[step], meta_recv.at[step], (target, core))

    def stat_copy(d):
        return remote(
            stat_s, statin_s.at[d - 1], stat_send.at[d - 1], stat_recv.at[d - 1],
            (here, lax.rem(core + d, cores)),
        )

    def column(row):
        return jnp.transpose(jnp.broadcast_to(row, (HEAD_DIM, rows)))

    doc_row = doc_ref[...].astype(F32)
    col_s[...] = column(doc_row)
    own_first = col_s[0:1, :]
    own_last = col_s[rows - 1 : rows, :]
    spans = [slice(i * TILE, (i + 1) * TILE) for i in range(count)]
    firsts = [col_s[i * TILE : i * TILE + 1, :] for i in range(count)]
    lasts = [col_s[(i + 1) * TILE - 1 : (i + 1) * TILE, :] for i in range(count)]
    for i, span in enumerate(spans):
        first_s[span, :] = same(col_s[span, :], firsts[i]).astype(BF16)
        last_s[span, :] = same(col_s[span, :], lasts[i]).astype(BF16)
    meta_s[0, 0:1, :] = own_first
    meta_s[0, 1:2, :] = own_last
    meta_s[0, 2:8, :] = jnp.zeros((6, HEAD_DIM), F32)

    total = 1 + 1 + (cores - 1) + has_up.astype(jnp.int32) + has_down.astype(jnp.int32)
    pl.semaphore_wait(barrier, total)
    meta_copy(0).start()

    def own_ahead(h):
        running = None
        for i, span in enumerate(spans):
            state = dot_tn(k_s[h, span, :] * last_s[span, :], v_s[h, span, :])
            if i > 0:
                enter_s[0, h, i] = same(lasts[i - 1], firsts[i]) * running
                state = state + same(lasts[i - 1], lasts[i]) * running
            running = state
        own_s[0, h] = running

    pair = 2 if heads % 2 == 0 else 1

    @pl.loop(0, heads // pair)
    def _(step):
        group = [step * pair + i for i in range(pair)]
        for h in group:
            load(0, h).wait()
            load(1, h).wait()
        for h in group:
            own_ahead(h)
        for h in group:
            state_copy(0, 0, h).start()

    ahead = lax.broadcasted_iota(jnp.int32, (TILE, HEAD_DIM), 0)
    lane = lax.broadcasted_iota(jnp.int32, (TILE, HEAD_DIM), 1)
    for i, span in enumerate(spans):
        col = col_s[span, :]
        for at in range(0, TILE, HEAD_DIM):
            start = i * TILE + at
            equal = col == doc_row[:, start : start + HEAD_DIM]
            mask_s[span, at : at + HEAD_DIM] = jnp.where(equal & (ahead >= lane + at), 1.0, 0.0).astype(BF16)
            maskt_s[span, at : at + HEAD_DIM] = jnp.where(equal & (ahead <= lane + at), 1.0, 0.0).astype(BF16)

    lang_row = lang_ref[...]
    weight_row = jnp.zeros((1, rows), F32)
    for i in range(table_ref.shape[0]):
        weight_row = jnp.where(lang_row == i, table_ref[i], weight_row)

    meta_copy(0).wait_recv()
    near_first = meta_s[1, 0:1, :]
    near_last = meta_s[1, 1:2, :]
    pair_first = jnp.where(bit_x == 0, own_first, near_first)
    pair_last = jnp.where(bit_x == 0, near_last, own_last)
    meta_s[2, 0:1, :] = pair_first
    meta_s[2, 1:2, :] = pair_last
    meta_s[2, 2:8, :] = jnp.zeros((6, HEAD_DIM), F32)
    meta_copy(1).start()
    sq_s[...] = jnp.zeros_like(sq_s)
    mx_s[...] = jnp.zeros_like(mx_s)
    meta_copy(1).wait_recv()
    other_first = meta_s[3, 0:1, :]
    other_last = meta_s[3, 1:2, :]
    group_first = jnp.where(bit_y == 0, pair_first, other_first)
    group_last = jnp.where(bit_y == 0, other_last, pair_last)
    meta_s[4, 0:1, :] = group_first
    meta_s[4, 1:2, :] = group_last
    meta_s[4, 2:8, :] = jnp.zeros((6, HEAD_DIM), F32)

    @pl.when(has_up)
    def _():
        meta_copy(2).start()

    @pl.when(has_down)
    def _():
        meta_copy(3).start()

    def factors(x, y, mine, target, theirs, other, group):
        x_on = x.astype(F32)
        y_on = y.astype(F32)
        equal = same(mine, theirs)
        pair = (jnp.where(x == 1, 1.0, equal), jnp.where(x == 1, equal, 1.0))
        take = (x_on * same(theirs, target), y_on * same(other, target))
        send = (same(mine, group), (1.0 - x_on) * same(theirs, group), 1.0 - y_on)
        return pair, take, send

    ahead_w = factors(bit_x, bit_y, own_last, own_first, near_last, other_last, group_last)
    back_w = factors(1 - bit_x, 1 - bit_y, own_first, own_last, near_first, other_first, group_first)

    def step_x(back, h):
        pair = (back_w if back else ahead_w)[0]
        state_copy(back, 0, h).wait_recv()
        pair_s[back, h] = pair[0] * own_s[back, h] + pair[1] * xin_s[back, h]
        state_copy(back, 1, h).start()

    def step_y(back, h):
        take, send = (back_w if back else ahead_w)[1:]
        state_copy(back, 1, h).wait_recv()
        near_state = xin_s[back, h]
        far_state = yin_s[back, h]
        send_s[back, h] = send[0] * own_s[back, h] + send[1] * near_state + send[2] * far_state

        @pl.when(has_down if back else has_up)
        def _():
            state_copy(back, 2, h).start()

        carry_s[back, h] = take[0] * near_state + take[1] * far_state

    def step_z(back, h):
        target = own_last if back else own_first

        @pl.when(has_up if back else has_down)
        def _():
            if back:
                end = meta_s[6, 0:1, :]
            else:
                end = meta_s[5, 1:2, :]
            state_copy(back, 2, h).wait_recv()
            carry_s[back, h] += same(end, target) * zin_s[back, h]

    @pl.when(has_down)
    def _():
        meta_copy(2).wait_recv()

    @pl.when(has_up)
    def _():
        meta_copy(3).wait_recv()

    def ahead_local(t):
        for span in spans:
            scores = dot_nt(q_s[t, span, :], k_s[t, span, :]).astype(BF16) * mask_s[span, :]
            part_s[t, span, :] = dot_nn(scores, v_s[t, span, :])
            turned = dot_nt(k_s[t, span, :], q_s[t, span, :]).astype(BF16)
            st_s[t, span, :] = turned * maskt_s[span, :]

    def ahead_finish(h):
        incoming = carry_s[0, h]
        gain = gain_ref[:, lanes(h)]
        for i, span in enumerate(spans):
            state = incoming
            if i > 0:
                state = enter_s[0, h, i] + same(firsts[i], own_first) * incoming
            state = state.astype(BF16)
            inc_s[h, i] = state
            out = part_s[h, span, :] + dot_nn(q_s[h, span, :] * first_s[span, :], state)
            out_s[h, span, :] = out
            sq_s[span, :] += out * out
            mx_s[span, :] += c_s[h, span, :].astype(F32) * gain * out

    def run(back, local_part, finish):
        bounds = sorted({0, heads, LAG_Z, heads + LAG_Z})
        for begin, end in zip(bounds[:-1], bounds[1:]):
            with_local = end <= heads
            with_finish = begin >= LAG_Z

            @pl.loop(begin, end)
            def _(t):
                if with_local:
                    if not back:
                        load(2, t).wait()
                        load(3, t).wait()
                    step_x(back, t)

                @pl.when((t >= LAG_Y) & (t < heads + LAG_Y))
                def _():
                    step_y(back, t - LAG_Y)

                if with_finish:
                    step_z(back, t - LAG_Z)
                    finish(t - LAG_Z)
                if with_local:
                    local_part(t)

    run(0, ahead_local, ahead_finish)

    stat_s[0:1, :] = jnp.sum(jnp.transpose(sq_s[...]), axis=0, keepdims=True)
    stat_s[1:2, :] = jnp.sum(jnp.transpose(mx_s[...]), axis=0, keepdims=True)
    stat_s[2:8, :] = jnp.zeros((6, rows), F32)
    for d in range(1, cores):
        stat_copy(d).start()
    squares = stat_s[0:1, :]
    mixed = stat_s[1:2, :]
    for d in range(1, cores):
        stat_copy(d).wait_recv()
        squares = squares + statin_s[d - 1, 0:1, :]
        mixed = mixed + statin_s[d - 1, 1:2, :]
    inv_rms = lax.rsqrt(squares / norm_width + EPSILON)
    sq_s[...] = column(inv_rms * weight_row)
    mx_s[...] = column(inv_rms * inv_rms * inv_rms * (mixed * weight_row) / norm_width)

    def own_back(h):
        gain = gain_ref[:, lanes(h)]
        running = None
        for i in reversed(range(count)):
            span = spans[i]
            grad = c_s[h, span, :].astype(F32) * gain * sq_s[span, :] - out_s[h, span, :] * mx_s[span, :]
            grad = grad.astype(BF16)
            g_s[h, span, :] = grad
            state = dot_tn(q_s[h, span, :] * first_s[span, :], grad)
            if i < count - 1:
                enter_s[1, h, i] = same(firsts[i + 1], lasts[i]) * running
                state = state + same(firsts[i + 1], firsts[i]) * running
            running = state
        own_s[1, h] = running

    @pl.loop(0, heads // pair)
    def _(step):
        group = [step * pair + i for i in range(pair)]
        for h in group:
            own_back(h)
        for h in group:
            state_copy(1, 0, h).start()

    def back_local(t):
        for i, span in enumerate(spans):
            scores = dot_nt(g_s[t, span, :], v_s[t, span, :]).astype(BF16) * mask_s[span, :]
            grad_q = dot_nn(scores, k_s[t, span, :])
            grad_q += dot_nt(g_s[t, span, :] * first_s[span, :], inc_s[t, i])
            dq_ref[span, lanes(t)] = grad_q.astype(BF16)
            turned = dot_nt(v_s[t, span, :], g_s[t, span, :]).astype(BF16) * maskt_s[span, :]
            part_s[t, span, :] = dot_nn(turned, q_s[t, span, :])
            dv_s[t, span, :] = dot_nn(st_s[t, span, :], g_s[t, span, :])

    def back_finish(h):
        returning = carry_s[1, h]
        for i, span in enumerate(spans):
            state = returning
            if i < count - 1:
                state = enter_s[1, h, i] + same(lasts[i], own_last) * returning
            state = state.astype(BF16)
            grad_k = part_s[h, span, :] + dot_nt(v_s[h, span, :] * last_s[span, :], state)
            dk_ref[span, lanes(h)] = grad_k.astype(BF16)
            grad_v = dv_s[h, span, :] + dot_nn(k_s[h, span, :] * last_s[span, :], state)
            dv_ref[span, lanes(h)] = grad_v.astype(BF16)

    run(1, back_local, back_finish)

    @pl.loop(0, heads)
    def _(h):
        for back in range(2):
            state_copy(back, 0, h).wait_send()
            state_copy(back, 1, h).wait_send()

            @pl.when(has_down if back else has_up)
            def _():
                state_copy(back, 2, h).wait_send()

    meta_copy(0).wait_send()
    meta_copy(1).wait_send()

    @pl.when(has_up)
    def _():
        meta_copy(2).wait_send()

    @pl.when(has_down)
    def _():
        meta_copy(3).wait_send()

    for d in range(1, cores):
        stat_copy(d).wait_send()


def write_out(a_ref, b_ref, c_ref, a_out, b_out, c_out, sem):
    pairs = ((a_ref, a_out), (b_ref, b_out), (c_ref, c_out))
    copies = [pltpu.make_async_copy(src, dst, sem.at[i]) for i, (src, dst) in enumerate(pairs)]
    for copy in copies:
        copy.start()
    for copy in copies:
        copy.wait()


def local(blocks, cores, query_vec, key_vec, value_vec, cotangent, norm_gain, doc_ids, lang_ids, loss_table):
    rows, cols = query_vec.shape
    heads = cols // HEAD_DIM
    count = rows // TILE
    state = (2, heads, HEAD_DIM, HEAD_DIM)
    per_head = (heads, rows, HEAD_DIM)
    any_spec = pl.BlockSpec(memory_space=pl.ANY)
    hbm_spec = pl.BlockSpec(memory_space=pltpu.HBM)
    vmem_spec = pl.BlockSpec(memory_space=pltpu.VMEM)
    operands = (
        loss_table,
        doc_ids.reshape(1, rows),
        lang_ids.reshape(1, rows),
        norm_gain.reshape(1, cols),
        query_vec,
        key_vec,
        value_vec,
        cotangent,
    )
    grads = pl.pallas_call(
        functools.partial(kernel, blocks, cores, HEADS * HEAD_DIM),
        out_shape=(pltpu.VMEM((rows, cols), BF16),) * 3,
        in_specs=[pl.BlockSpec(memory_space=pltpu.SMEM)] + [vmem_spec] * 3 + [hbm_spec] * 4,
        out_specs=(vmem_spec,) * 3,
        scratch_shapes=[pltpu.VMEM(per_head, BF16)] * 5
        + [pltpu.VMEM(per_head, F32)] * 3
        + [pltpu.VMEM((heads, rows, TILE), BF16)]
        + [pltpu.VMEM((rows, TILE), BF16)] * 2
        + [pltpu.VMEM(state, F32)] * 7
        + [
            pltpu.VMEM((heads, count) + state[2:], BF16),
            pltpu.VMEM((2, heads, count) + state[2:], F32),
            pltpu.VMEM((rows, HEAD_DIM), F32),
            pltpu.VMEM((rows, HEAD_DIM), BF16),
            pltpu.VMEM((rows, HEAD_DIM), BF16),
            pltpu.VMEM((rows, HEAD_DIM), F32),
            pltpu.VMEM((rows, HEAD_DIM), F32),
            pltpu.VMEM((8, rows), F32),
            pltpu.VMEM((max(cores - 1, 1), 8, rows), F32),
            pltpu.VMEM((7, 8, HEAD_DIM), F32),
            pltpu.SemaphoreType.DMA((4, heads)),
            pltpu.SemaphoreType.DMA((2, 3, heads)),
            pltpu.SemaphoreType.DMA((2, 3, heads)),
            pltpu.SemaphoreType.DMA((4,)),
            pltpu.SemaphoreType.DMA((4,)),
            pltpu.SemaphoreType.DMA((max(cores - 1, 1),)),
            pltpu.SemaphoreType.DMA((max(cores - 1, 1),)),
        ],
        compiler_params=pltpu.CompilerParams(
            collective_id=0, has_side_effects=True, vmem_limit_bytes=VMEM_BYTES
        ),
    )(
        *(pltpu.with_memory_space_constraint(x, pltpu.HBM) for x in operands),
    )
    shape = jax.ShapeDtypeStruct((rows, cols), BF16)
    return pl.pallas_call(
        write_out,
        out_shape=(shape,) * 3,
        in_specs=[any_spec] * 3,
        out_specs=(any_spec,) * 3,
        scratch_shapes=[pltpu.SemaphoreType.DMA((3,))],
    )(*grads)


def solution(mesh):
    sizes = dict(mesh.shape)
    in_specs = (
        P("seq", "head"),
        P("seq", "head"),
        P("seq", "head"),
        P("seq", "head"),
        P("head"),
        P("seq"),
        P("seq"),
        P(),
    )
    out_specs = (P("seq", "head"), P("seq", "head"), P("seq", "head"))
    body = functools.partial(local, sizes["seq"], sizes["head"])
    return jax.shard_map(body, mesh=mesh, in_specs=in_specs, out_specs=out_specs, check_vma=False)
```

```python
import functools

import jax
import jax.numpy as jnp
from jax import lax
from jax.experimental import pallas as pl
from jax.experimental.pallas import tpu as pltpu
from jax.sharding import PartitionSpec as P

HEAD_DIM = 128
HEADS = 16
EPSILON = 1e-06
TILE = 256
LAG_Y = 2
PIECES = 4
LAG_Z = 6
VMEM_BYTES = 44 * 2**20
MESH = pl.DeviceIdType.MESH
F32 = jnp.float32
BF16 = jnp.bfloat16


def dot_nn(a, b):
    return lax.dot_general(a, b, (((1,), (0,)), ((), ())), preferred_element_type=F32)


def dot_nt(a, b):
    return lax.dot_general(a, b, (((1,), (1,)), ((), ())), preferred_element_type=F32)


def dot_tn(a, b):
    return lax.dot_general(a, b, (((0,), (0,)), ((), ())), preferred_element_type=F32)


def same(a, b):
    return jnp.where(a == b, 1.0, 0.0)


def kernel(
    blocks, cores, norm_width,
    table_ref, doc_ref, lang_ref, gain_ref, q_hbm, k_hbm, v_hbm, c_hbm,
    dq_ref, dk_ref, dv_ref,
    q_s, k_s, v_s, c_s, g_s, out_s, part_s, dv_s, st_s, mask_s, maskt_s,
    own_s, xin_s, pair_s, yin_s, send_s, zin_s, carry_s, inc_s, enter_s,
    col_s, first_s, last_s, sq_s, mx_s, stat_s, statin_s, meta_s,
    in_sem, comm_send, comm_recv, meta_send, meta_recv, stat_send, stat_recv,
):
    heads, rows, _ = q_s.shape
    count = rows // TILE
    here = lax.axis_index("seq")
    core = lax.axis_index("head")
    bit_x = lax.rem(here, 2)
    bit_y = lax.rem(here // 2, 2)
    near = here + 1 - 2 * bit_x
    across = here + 2 - 4 * bit_y
    has_up = here + 4 < blocks
    has_down = here >= 4
    up = jnp.where(has_up, here + 4, here - 4)
    down = jnp.where(has_down, here - 4, here + 4)

    def load(which, h):
        src = (k_hbm, v_hbm, q_hbm, c_hbm)[which]
        dst = (k_s, v_s, q_s, c_s)[which]
        at = pl.ds(pl.multiple_of(h * HEAD_DIM, HEAD_DIM), HEAD_DIM)
        return pltpu.make_async_copy(src.at[:, at], dst.at[h], in_sem.at[which, h])

    def lanes(h):
        return pl.ds(pl.multiple_of(h * HEAD_DIM, HEAD_DIM), HEAD_DIM)

    for group in ((0, 1), (2, 3)):
        for h in range(heads):
            for which in group:
                load(which, h).start()

    barrier = pltpu.get_barrier_semaphore()

    def greet(device):
        pl.semaphore_signal(barrier, inc=1, device_id=device, device_id_type=MESH)

    greet((near, core))
    greet((across, core))
    for d in range(1, cores):
        greet((here, lax.rem(core + d, cores)))

    @pl.when(has_up)
    def _():
        greet((up, core))

    @pl.when(has_down)
    def _():
        greet((down, core))

    def remote(src, dst, send_sem, recv_sem, device):
        return pltpu.make_async_remote_copy(
            src_ref=src, dst_ref=dst, send_sem=send_sem, recv_sem=recv_sem,
            device_id=device, device_id_type=MESH,
        )

    def state_copy(back, step, h):
        src = (own_s, pair_s, send_s)[step].at[back, h]
        dst = (xin_s, yin_s, zin_s)[step].at[back, h]
        target = (near, across, down if back else up)[step]
        return remote(
            src, dst, comm_send.at[back, step, h], comm_recv.at[back, step, h], (target, core)
        )

    def meta_copy(step):
        target = (near, across, up, down)[step]
        src = meta_s.at[(0, 2, 4, 4)[step]]
        dst = meta_s.at[(1, 3, 5, 6)[step]]
        return remote(src, dst, meta_send.at[step], meta_recv.at[step], (target, core))

    def stat_copy(d):
        return remote(
            stat_s, statin_s.at[d - 1], stat_send.at[d - 1], stat_recv.at[d - 1],
            (here, lax.rem(core + d, cores)),
        )

    def column(row):
        return jnp.transpose(jnp.broadcast_to(row, (HEAD_DIM, rows)))

    doc_row = doc_ref[...].astype(F32)
    col_s[...] = column(doc_row)
    own_first = col_s[0:1, :]
    own_last = col_s[rows - 1 : rows, :]
    spans = [slice(i * TILE, (i + 1) * TILE) for i in range(count)]
    firsts = [col_s[i * TILE : i * TILE + 1, :] for i in range(count)]
    lasts = [col_s[(i + 1) * TILE - 1 : (i + 1) * TILE, :] for i in range(count)]
    for i, span in enumerate(spans):
        first_s[span, :] = same(col_s[span, :], firsts[i]).astype(BF16)
        last_s[span, :] = same(col_s[span, :], lasts[i]).astype(BF16)
    meta_s[0, 0:1, :] = own_first
    meta_s[0, 1:2, :] = own_last
    meta_s[0, 2:8, :] = jnp.zeros((6, HEAD_DIM), F32)

    total = 1 + 1 + (cores - 1) + has_up.astype(jnp.int32) + has_down.astype(jnp.int32)
    pl.semaphore_wait(barrier, total)
    meta_copy(0).start()

    def own_ahead(h):
        running = None
        for i, span in enumerate(spans):
            state = dot_tn(k_s[h, span, :] * last_s[span, :], v_s[h, span, :])
            if i > 0:
                enter_s[0, h, i] = same(lasts[i - 1], firsts[i]) * running
                state = state + same(lasts[i - 1], lasts[i]) * running
            running = state
        own_s[0, h] = running

    pair = 2 if heads % 2 == 0 else 1

    @pl.loop(0, heads // pair)
    def _(step):
        group = [step * pair + i for i in range(pair)]
        for h in group:
            load(0, h).wait()
            load(1, h).wait()
        for h in group:
            own_ahead(h)
        for h in group:
            state_copy(0, 0, h).start()

    ahead = lax.broadcasted_iota(jnp.int32, (TILE, HEAD_DIM), 0)
    lane = lax.broadcasted_iota(jnp.int32, (TILE, HEAD_DIM), 1)
    for i, span in enumerate(spans):
        col = col_s[span, :]
        for at in range(0, TILE, HEAD_DIM):
            start = i * TILE + at
            equal = col == doc_row[:, start : start + HEAD_DIM]
            mask_s[span, at : at + HEAD_DIM] = jnp.where(equal & (ahead >= lane + at), 1.0, 0.0).astype(BF16)
            maskt_s[span, at : at + HEAD_DIM] = jnp.where(equal & (ahead <= lane + at), 1.0, 0.0).astype(BF16)

    lang_row = lang_ref[...]
    weight_row = jnp.zeros((1, rows), F32)
    for i in range(table_ref.shape[0]):
        weight_row = jnp.where(lang_row == i, table_ref[i], weight_row)

    meta_copy(0).wait_recv()
    near_first = meta_s[1, 0:1, :]
    near_last = meta_s[1, 1:2, :]
    pair_first = jnp.where(bit_x == 0, own_first, near_first)
    pair_last = jnp.where(bit_x == 0, near_last, own_last)
    meta_s[2, 0:1, :] = pair_first
    meta_s[2, 1:2, :] = pair_last
    meta_s[2, 2:8, :] = jnp.zeros((6, HEAD_DIM), F32)
    meta_copy(1).start()
    sq_s[...] = jnp.zeros_like(sq_s)
    mx_s[...] = jnp.zeros_like(mx_s)
    meta_copy(1).wait_recv()
    other_first = meta_s[3, 0:1, :]
    other_last = meta_s[3, 1:2, :]
    group_first = jnp.where(bit_y == 0, pair_first, other_first)
    group_last = jnp.where(bit_y == 0, other_last, pair_last)
    meta_s[4, 0:1, :] = group_first
    meta_s[4, 1:2, :] = group_last
    meta_s[4, 2:8, :] = jnp.zeros((6, HEAD_DIM), F32)

    @pl.when(has_up)
    def _():
        meta_copy(2).start()

    @pl.when(has_down)
    def _():
        meta_copy(3).start()

    def factors(x, y, mine, target, theirs, other, group):
        x_on = x.astype(F32)
        y_on = y.astype(F32)
        equal = same(mine, theirs)
        pair = (jnp.where(x == 1, 1.0, equal), jnp.where(x == 1, equal, 1.0))
        take = (x_on * same(theirs, target), y_on * same(other, target))
        send = (same(mine, group), (1.0 - x_on) * same(theirs, group), 1.0 - y_on)
        return pair, take, send

    ahead_w = factors(bit_x, bit_y, own_last, own_first, near_last, other_last, group_last)
    back_w = factors(1 - bit_x, 1 - bit_y, own_first, own_last, near_first, other_first, group_first)

    def step_x(back, h):
        pair = (back_w if back else ahead_w)[0]
        state_copy(back, 0, h).wait_recv()
        pair_s[back, h] = pair[0] * own_s[back, h] + pair[1] * xin_s[back, h]
        state_copy(back, 1, h).start()

    def step_y(back, h):
        take, send = (back_w if back else ahead_w)[1:]
        state_copy(back, 1, h).wait_recv()
        near_state = xin_s[back, h]
        far_state = yin_s[back, h]
        send_s[back, h] = send[0] * own_s[back, h] + send[1] * near_state + send[2] * far_state

        @pl.when(has_down if back else has_up)
        def _():
            state_copy(back, 2, h).start()

        carry_s[back, h] = take[0] * near_state + take[1] * far_state

    def step_z(back, h):
        target = own_last if back else own_first

        @pl.when(has_up if back else has_down)
        def _():
            if back:
                end = meta_s[6, 0:1, :]
            else:
                end = meta_s[5, 1:2, :]
            state_copy(back, 2, h).wait_recv()
            carry_s[back, h] += same(end, target) * zin_s[back, h]

    @pl.when(has_down)
    def _():
        meta_copy(2).wait_recv()

    @pl.when(has_up)
    def _():
        meta_copy(3).wait_recv()

    def ahead_local(t):
        for span in spans:
            scores = dot_nt(q_s[t, span, :], k_s[t, span, :]).astype(BF16) * mask_s[span, :]
            part_s[t, span, :] = dot_nn(scores, v_s[t, span, :])
            turned = dot_nt(k_s[t, span, :], q_s[t, span, :]).astype(BF16)
            st_s[t, span, :] = turned * maskt_s[span, :]

    def ahead_finish(h):
        incoming = carry_s[0, h]
        gain = gain_ref[:, lanes(h)]
        for i, span in enumerate(spans):
            state = incoming
            if i > 0:
                state = enter_s[0, h, i] + same(firsts[i], own_first) * incoming
            state = state.astype(BF16)
            inc_s[h, i] = state
            out = part_s[h, span, :] + dot_nn(q_s[h, span, :] * first_s[span, :], state)
            out_s[h, span, :] = out
            sq_s[span, :] += out * out
            mx_s[span, :] += c_s[h, span, :].astype(F32) * gain * out

    def run(back, local_part, finish):
        bounds = sorted({0, heads, LAG_Z, heads + LAG_Z})
        for begin, end in zip(bounds[:-1], bounds[1:]):
            with_local = end <= heads
            with_finish = begin >= LAG_Z

            @pl.loop(begin, end)
            def _(t):
                if with_local:
                    if not back:
                        load(2, t).wait()
                        load(3, t).wait()
                    step_x(back, t)

                @pl.when((t >= LAG_Y) & (t < heads + LAG_Y))
                def _():
                    step_y(back, t - LAG_Y)

                if with_finish:
                    step_z(back, t - LAG_Z)
                    finish(t - LAG_Z)
                if with_local:
                    local_part(t)

    run(0, ahead_local, ahead_finish)

    stat_s[0:1, :] = jnp.sum(jnp.transpose(sq_s[...]), axis=0, keepdims=True)
    stat_s[1:2, :] = jnp.sum(jnp.transpose(mx_s[...]), axis=0, keepdims=True)
    stat_s[2:8, :] = jnp.zeros((6, rows), F32)
    for d in range(1, cores):
        stat_copy(d).start()
    squares = stat_s[0:1, :]
    mixed = stat_s[1:2, :]
    for d in range(1, cores):
        stat_copy(d).wait_recv()
        squares = squares + statin_s[d - 1, 0:1, :]
        mixed = mixed + statin_s[d - 1, 1:2, :]
    inv_rms = lax.rsqrt(squares / norm_width + EPSILON)
    sq_s[...] = column(inv_rms * weight_row)
    mx_s[...] = column(inv_rms * inv_rms * inv_rms * (mixed * weight_row) / norm_width)

    def own_back(h):
        gain = gain_ref[:, lanes(h)]
        running = None
        for i in reversed(range(count)):
            span = spans[i]
            grad = c_s[h, span, :].astype(F32) * gain * sq_s[span, :] - out_s[h, span, :] * mx_s[span, :]
            grad = grad.astype(BF16)
            g_s[h, span, :] = grad
            state = dot_tn(q_s[h, span, :] * first_s[span, :], grad)
            if i < count - 1:
                enter_s[1, h, i] = same(firsts[i + 1], lasts[i]) * running
                state = state + same(firsts[i + 1], firsts[i]) * running
            running = state
        own_s[1, h] = running

    @pl.loop(0, heads // pair)
    def _(step):
        group = [step * pair + i for i in range(pair)]
        for h in group:
            own_back(h)
        for h in group:
            state_copy(1, 0, h).start()

    def back_local(t):
        for i, span in enumerate(spans):
            scores = dot_nt(g_s[t, span, :], v_s[t, span, :]).astype(BF16) * mask_s[span, :]
            grad_q = dot_nn(scores, k_s[t, span, :])
            grad_q += dot_nt(g_s[t, span, :] * first_s[span, :], inc_s[t, i])
            dq_ref[span, lanes(t)] = grad_q.astype(BF16)
            turned = dot_nt(v_s[t, span, :], g_s[t, span, :]).astype(BF16) * maskt_s[span, :]
            part_s[t, span, :] = dot_nn(turned, q_s[t, span, :])
            dv_s[t, span, :] = dot_nn(st_s[t, span, :], g_s[t, span, :])

    def back_finish(h):
        returning = carry_s[1, h]
        for i, span in enumerate(spans):
            state = returning
            if i < count - 1:
                state = enter_s[1, h, i] + same(lasts[i], own_last) * returning
            state = state.astype(BF16)
            grad_k = part_s[h, span, :] + dot_nt(v_s[h, span, :] * last_s[span, :], state)
            dk_ref[span, lanes(h)] = grad_k.astype(BF16)
            grad_v = dv_s[h, span, :] + dot_nn(k_s[h, span, :] * last_s[span, :], state)
            dv_ref[span, lanes(h)] = grad_v.astype(BF16)

    run(1, back_local, back_finish)

    @pl.loop(0, heads)
    def _(h):
        for back in range(2):
            state_copy(back, 0, h).wait_send()
            state_copy(back, 1, h).wait_send()

            @pl.when(has_down if back else has_up)
            def _():
                state_copy(back, 2, h).wait_send()

    meta_copy(0).wait_send()
    meta_copy(1).wait_send()

    @pl.when(has_up)
    def _():
        meta_copy(2).wait_send()

    @pl.when(has_down)
    def _():
        meta_copy(3).wait_send()

    for d in range(1, cores):
        stat_copy(d).wait_send()


def write_out(a_ref, b_ref, c_ref, a_out, b_out, c_out, sem):
    rows = a_ref.shape[0] // PIECES
    copies = []
    for i, (src, dst) in enumerate(((a_ref, a_out), (b_ref, b_out), (c_ref, c_out))):
        for j in range(PIECES):
            part = slice(j * rows, (j + 1) * rows)
            copies.append(pltpu.make_async_copy(src.at[part], dst.at[part], sem.at[i * PIECES + j]))
    for copy in copies:
        copy.start()
    for copy in copies:
        copy.wait()


def local(blocks, cores, query_vec, key_vec, value_vec, cotangent, norm_gain, doc_ids, lang_ids, loss_table):
    rows, cols = query_vec.shape
    heads = cols // HEAD_DIM
    count = rows // TILE
    state = (2, heads, HEAD_DIM, HEAD_DIM)
    per_head = (heads, rows, HEAD_DIM)
    any_spec = pl.BlockSpec(memory_space=pl.ANY)
    hbm_spec = pl.BlockSpec(memory_space=pltpu.HBM)
    vmem_spec = pl.BlockSpec(memory_space=pltpu.VMEM)
    operands = (
        loss_table,
        doc_ids.reshape(1, rows),
        lang_ids.reshape(1, rows),
        norm_gain.reshape(1, cols),
        query_vec,
        key_vec,
        value_vec,
        cotangent,
    )
    grads = pl.pallas_call(
        functools.partial(kernel, blocks, cores, HEADS * HEAD_DIM),
        out_shape=(pltpu.VMEM((rows, cols), BF16),) * 3,
        in_specs=[pl.BlockSpec(memory_space=pltpu.SMEM)] + [vmem_spec] * 3 + [hbm_spec] * 4,
        out_specs=(vmem_spec,) * 3,
        scratch_shapes=[pltpu.VMEM(per_head, BF16)] * 5
        + [pltpu.VMEM(per_head, F32)] * 3
        + [pltpu.VMEM((heads, rows, TILE), BF16)]
        + [pltpu.VMEM((rows, TILE), BF16)] * 2
        + [pltpu.VMEM(state, F32)] * 7
        + [
            pltpu.VMEM((heads, count) + state[2:], BF16),
            pltpu.VMEM((2, heads, count) + state[2:], F32),
            pltpu.VMEM((rows, HEAD_DIM), F32),
            pltpu.VMEM((rows, HEAD_DIM), BF16),
            pltpu.VMEM((rows, HEAD_DIM), BF16),
            pltpu.VMEM((rows, HEAD_DIM), F32),
            pltpu.VMEM((rows, HEAD_DIM), F32),
            pltpu.VMEM((8, rows), F32),
            pltpu.VMEM((max(cores - 1, 1), 8, rows), F32),
            pltpu.VMEM((7, 8, HEAD_DIM), F32),
            pltpu.SemaphoreType.DMA((4, heads)),
            pltpu.SemaphoreType.DMA((2, 3, heads)),
            pltpu.SemaphoreType.DMA((2, 3, heads)),
            pltpu.SemaphoreType.DMA((4,)),
            pltpu.SemaphoreType.DMA((4,)),
            pltpu.SemaphoreType.DMA((max(cores - 1, 1),)),
            pltpu.SemaphoreType.DMA((max(cores - 1, 1),)),
        ],
        compiler_params=pltpu.CompilerParams(
            collective_id=0, has_side_effects=True, vmem_limit_bytes=VMEM_BYTES
        ),
    )(
        *(pltpu.with_memory_space_constraint(x, pltpu.HBM) for x in operands),
    )
    shape = jax.ShapeDtypeStruct((rows, cols), BF16)
    return pl.pallas_call(
        write_out,
        out_shape=(shape,) * 3,
        in_specs=[vmem_spec] * 3,
        out_specs=(any_spec,) * 3,
        scratch_shapes=[pltpu.SemaphoreType.DMA((3 * PIECES,))],
        compiler_params=pltpu.CompilerParams(vmem_limit_bytes=8 * 2**20),
    )(*(pltpu.with_memory_space_constraint(x, pltpu.VMEM) for x in grads))


def solution(mesh):
    sizes = dict(mesh.shape)
    in_specs = (
        P("seq", "head"),
        P("seq", "head"),
        P("seq", "head"),
        P("seq", "head"),
        P("head"),
        P("seq"),
        P("seq"),
        P(),
    )
    out_specs = (P("seq", "head"), P("seq", "head"), P("seq", "head"))
    body = functools.partial(local, sizes["seq"], sizes["head"])
    return jax.shard_map(body, mesh=mesh, in_specs=in_specs, out_specs=out_specs, check_vma=False)
```

```python
import functools

import jax
import jax.numpy as jnp
from jax import lax
from jax.experimental import pallas as pl
from jax.experimental.pallas import tpu as pltpu
from jax.sharding import PartitionSpec as P

HEAD_DIM = 128
HEADS = 16
EPSILON = 1e-06
TILE = 256
PART = 64
LAG_Y = 2
PIECES = 4
LAG_Z = 6
VMEM_BYTES = 44 * 2**20
MESH = pl.DeviceIdType.MESH
F32 = jnp.float32
BF16 = jnp.bfloat16


def dot_nn(a, b):
    return lax.dot_general(a, b, (((1,), (0,)), ((), ())), preferred_element_type=F32)


def dot_nt(a, b):
    return lax.dot_general(a, b, (((1,), (1,)), ((), ())), preferred_element_type=F32)


def dot_tn(a, b):
    return lax.dot_general(a, b, (((0,), (0,)), ((), ())), preferred_element_type=F32)


def same(a, b):
    return jnp.where(a == b, 1.0, 0.0)


def kernel(
    blocks, cores, norm_width,
    table_hbm, doc_hbm, lang_hbm, gain_hbm, q_hbm, k_hbm, v_hbm, c_hbm,
    dq_ref, dk_ref, dv_ref,
    table_ref, doc_ref, lang_ref, gain_ref,
    q_s, k_s, v_s, c_s, g_s, out_s, part_s, dv_s, st_s, mask_s, maskt_s,
    own_s, xin_s, pair_s, yin_s, send_s, zin_s, carry_s, inc_s, enter_s,
    col_s, first_s, last_s, sq_s, mx_s, stat_s, statin_s, meta_s,
    small_sem, in_sem, comm_send, comm_recv, meta_send, meta_recv, stat_send, stat_recv,
):
    heads, rows, _ = q_s.shape
    count = rows // TILE
    here = lax.axis_index("seq")
    core = lax.axis_index("head")
    bit_x = lax.rem(here, 2)
    bit_y = lax.rem(here // 2, 2)
    near = here + 1 - 2 * bit_x
    across = here + 2 - 4 * bit_y
    has_up = here + 4 < blocks
    has_down = here >= 4
    up = jnp.where(has_up, here + 4, here - 4)
    down = jnp.where(has_down, here - 4, here + 4)

    def load(which, h):
        src = (k_hbm, v_hbm, q_hbm, c_hbm)[which]
        dst = (k_s, v_s, q_s, c_s)[which]
        at = pl.ds(pl.multiple_of(h * HEAD_DIM, HEAD_DIM), HEAD_DIM)
        return pltpu.make_async_copy(src.at[:, at], dst.at[h], in_sem.at[which, h])

    def lanes(h):
        return pl.ds(pl.multiple_of(h * HEAD_DIM, HEAD_DIM), HEAD_DIM)

    small = [
        pltpu.make_async_copy(src, dst, small_sem.at[i])
        for i, (src, dst) in enumerate(
            ((doc_hbm, doc_ref), (lang_hbm, lang_ref), (gain_hbm, gain_ref), (table_hbm, table_ref))
        )
    ]
    for copy in small:
        copy.start()
    for group in ((0, 1), (2, 3)):
        for h in range(heads):
            for which in group:
                load(which, h).start()

    barrier = pltpu.get_barrier_semaphore()

    def greet(device):
        pl.semaphore_signal(barrier, inc=1, device_id=device, device_id_type=MESH)

    greet((near, core))
    greet((across, core))
    for d in range(1, cores):
        greet((here, lax.rem(core + d, cores)))

    @pl.when(has_up)
    def _():
        greet((up, core))

    @pl.when(has_down)
    def _():
        greet((down, core))

    def remote(src, dst, send_sem, recv_sem, device):
        return pltpu.make_async_remote_copy(
            src_ref=src, dst_ref=dst, send_sem=send_sem, recv_sem=recv_sem,
            device_id=device, device_id_type=MESH,
        )

    parts = [slice(i * PART, (i + 1) * PART) for i in range(HEAD_DIM // PART)]

    def state_copy(back, step, h, i):
        src = (own_s, pair_s, send_s)[step].at[back, h, parts[i]]
        dst = (xin_s, yin_s, zin_s)[step].at[back, h, parts[i]]
        target = (near, across, down if back else up)[step]
        return remote(
            src, dst, comm_send.at[back, step, h, i], comm_recv.at[back, step, h, i], (target, core)
        )

    def send_own(back, h):
        for i in range(len(parts)):
            state_copy(back, 0, h, i).start()

    def meta_copy(step):
        target = (near, across, up, down)[step]
        src = meta_s.at[(0, 2, 4, 4)[step]]
        dst = meta_s.at[(1, 3, 5, 6)[step]]
        return remote(src, dst, meta_send.at[step], meta_recv.at[step], (target, core))

    def stat_copy(d):
        return remote(
            stat_s, statin_s.at[d - 1], stat_send.at[d - 1], stat_recv.at[d - 1],
            (here, lax.rem(core + d, cores)),
        )

    def column(row):
        return jnp.transpose(jnp.broadcast_to(row, (HEAD_DIM, rows)))

    small[0].wait()
    doc_row = doc_ref[...].astype(F32)
    col_s[...] = column(doc_row)
    own_first = col_s[0:1, :]
    own_last = col_s[rows - 1 : rows, :]
    spans = [slice(i * TILE, (i + 1) * TILE) for i in range(count)]
    firsts = [col_s[i * TILE : i * TILE + 1, :] for i in range(count)]
    lasts = [col_s[(i + 1) * TILE - 1 : (i + 1) * TILE, :] for i in range(count)]
    for i, span in enumerate(spans):
        first_s[span, :] = same(col_s[span, :], firsts[i]).astype(BF16)
        last_s[span, :] = same(col_s[span, :], lasts[i]).astype(BF16)
    meta_s[0, 0:1, :] = own_first
    meta_s[0, 1:2, :] = own_last
    meta_s[0, 2:8, :] = jnp.zeros((6, HEAD_DIM), F32)

    total = 1 + 1 + (cores - 1) + has_up.astype(jnp.int32) + has_down.astype(jnp.int32)
    pl.semaphore_wait(barrier, total)
    meta_copy(0).start()

    def own_ahead(h):
        running = None
        for i, span in enumerate(spans):
            state = dot_tn(k_s[h, span, :] * last_s[span, :], v_s[h, span, :])
            if i > 0:
                enter_s[0, h, i] = same(lasts[i - 1], firsts[i]) * running
                state = state + same(lasts[i - 1], lasts[i]) * running
            running = state
        own_s[0, h] = running

    pair = 2 if heads % 2 == 0 else 1

    @pl.loop(0, heads // pair)
    def _(step):
        group = [step * pair + i for i in range(pair)]
        for h in group:
            load(0, h).wait()
            load(1, h).wait()
        for h in group:
            own_ahead(h)
        for h in group:
            send_own(0, h)

    ahead = lax.broadcasted_iota(jnp.int32, (TILE, HEAD_DIM), 0)
    lane = lax.broadcasted_iota(jnp.int32, (TILE, HEAD_DIM), 1)
    for i, span in enumerate(spans):
        col = col_s[span, :]
        for at in range(0, TILE, HEAD_DIM):
            start = i * TILE + at
            equal = col == doc_row[:, start : start + HEAD_DIM]
            mask_s[span, at : at + HEAD_DIM] = jnp.where(equal & (ahead >= lane + at), 1.0, 0.0).astype(BF16)
            maskt_s[span, at : at + HEAD_DIM] = jnp.where(equal & (ahead <= lane + at), 1.0, 0.0).astype(BF16)

    for copy in small[1:]:
        copy.wait()
    lang_row = lang_ref[...]
    weight_row = jnp.zeros((1, rows), F32)
    for i in range(table_ref.shape[0]):
        weight_row = jnp.where(lang_row == i, table_ref[i], weight_row)

    meta_copy(0).wait_recv()
    near_first = meta_s[1, 0:1, :]
    near_last = meta_s[1, 1:2, :]
    pair_first = jnp.where(bit_x == 0, own_first, near_first)
    pair_last = jnp.where(bit_x == 0, near_last, own_last)
    meta_s[2, 0:1, :] = pair_first
    meta_s[2, 1:2, :] = pair_last
    meta_s[2, 2:8, :] = jnp.zeros((6, HEAD_DIM), F32)
    meta_copy(1).start()
    sq_s[...] = jnp.zeros_like(sq_s)
    mx_s[...] = jnp.zeros_like(mx_s)
    meta_copy(1).wait_recv()
    other_first = meta_s[3, 0:1, :]
    other_last = meta_s[3, 1:2, :]
    group_first = jnp.where(bit_y == 0, pair_first, other_first)
    group_last = jnp.where(bit_y == 0, other_last, pair_last)
    meta_s[4, 0:1, :] = group_first
    meta_s[4, 1:2, :] = group_last
    meta_s[4, 2:8, :] = jnp.zeros((6, HEAD_DIM), F32)

    @pl.when(has_up)
    def _():
        meta_copy(2).start()

    @pl.when(has_down)
    def _():
        meta_copy(3).start()

    def factors(x, y, mine, target, theirs, other, group):
        x_on = x.astype(F32)
        y_on = y.astype(F32)
        equal = same(mine, theirs)
        pair = (jnp.where(x == 1, 1.0, equal), jnp.where(x == 1, equal, 1.0))
        take = (x_on * same(theirs, target), y_on * same(other, target))
        send = (same(mine, group), (1.0 - x_on) * same(theirs, group), 1.0 - y_on)
        return pair, take, send

    ahead_w = factors(bit_x, bit_y, own_last, own_first, near_last, other_last, group_last)
    back_w = factors(1 - bit_x, 1 - bit_y, own_first, own_last, near_first, other_first, group_first)

    def step_x(back, h):
        pair = (back_w if back else ahead_w)[0]
        for i, part in enumerate(parts):
            state_copy(back, 0, h, i).wait_recv()
            pair_s[back, h, part] = pair[0] * own_s[back, h, part] + pair[1] * xin_s[back, h, part]
            state_copy(back, 1, h, i).start()

    def step_y(back, h):
        take, send = (back_w if back else ahead_w)[1:]
        for i, part in enumerate(parts):
            state_copy(back, 1, h, i).wait_recv()
            near_state = xin_s[back, h, part]
            far_state = yin_s[back, h, part]
            send_s[back, h, part] = send[0] * own_s[back, h, part] + send[1] * near_state + send[2] * far_state

            @pl.when(has_down if back else has_up)
            def _():
                state_copy(back, 2, h, i).start()

            carry_s[back, h, part] = take[0] * near_state + take[1] * far_state

    def step_z(back, h):
        target = own_last if back else own_first

        @pl.when(has_up if back else has_down)
        def _():
            if back:
                end = meta_s[6, 0:1, :]
            else:
                end = meta_s[5, 1:2, :]
            for i in range(len(parts)):
                state_copy(back, 2, h, i).wait_recv()
            carry_s[back, h] += same(end, target) * zin_s[back, h]

    @pl.when(has_down)
    def _():
        meta_copy(2).wait_recv()

    @pl.when(has_up)
    def _():
        meta_copy(3).wait_recv()

    def ahead_local(t):
        for span in spans:
            scores = dot_nt(q_s[t, span, :], k_s[t, span, :]).astype(BF16) * mask_s[span, :]
            part_s[t, span, :] = dot_nn(scores, v_s[t, span, :])
            turned = dot_nt(k_s[t, span, :], q_s[t, span, :]).astype(BF16)
            st_s[t, span, :] = turned * maskt_s[span, :]

    def ahead_finish(h):
        incoming = carry_s[0, h]
        gain = gain_ref[:, lanes(h)]
        for i, span in enumerate(spans):
            state = incoming
            if i > 0:
                state = enter_s[0, h, i] + same(firsts[i], own_first) * incoming
            state = state.astype(BF16)
            inc_s[h, i] = state
            out = part_s[h, span, :] + dot_nn(q_s[h, span, :] * first_s[span, :], state)
            out_s[h, span, :] = out
            sq_s[span, :] += out * out
            mx_s[span, :] += c_s[h, span, :].astype(F32) * gain * out

    def run(back, local_part, finish):
        bounds = sorted({0, heads, LAG_Z, heads + LAG_Z})
        for begin, end in zip(bounds[:-1], bounds[1:]):
            with_local = end <= heads
            with_finish = begin >= LAG_Z

            @pl.loop(begin, end)
            def _(t):
                @pl.when((t >= LAG_Y) & (t < heads + LAG_Y))
                def _():
                    step_y(back, t - LAG_Y)

                if with_local:
                    step_x(back, t)
                    if not back:
                        load(2, t).wait()
                        load(3, t).wait()

                if with_finish:
                    step_z(back, t - LAG_Z)
                    finish(t - LAG_Z)
                if with_local:
                    local_part(t)

    run(0, ahead_local, ahead_finish)

    stat_s[0:1, :] = jnp.sum(jnp.transpose(sq_s[...]), axis=0, keepdims=True)
    stat_s[1:2, :] = jnp.sum(jnp.transpose(mx_s[...]), axis=0, keepdims=True)
    stat_s[2:8, :] = jnp.zeros((6, rows), F32)
    for d in range(1, cores):
        stat_copy(d).start()
    squares = stat_s[0:1, :]
    mixed = stat_s[1:2, :]
    for d in range(1, cores):
        stat_copy(d).wait_recv()
        squares = squares + statin_s[d - 1, 0:1, :]
        mixed = mixed + statin_s[d - 1, 1:2, :]
    inv_rms = lax.rsqrt(squares / norm_width + EPSILON)
    sq_s[...] = column(inv_rms * weight_row)
    mx_s[...] = column(inv_rms * inv_rms * inv_rms * (mixed * weight_row) / norm_width)

    def own_back(h):
        gain = gain_ref[:, lanes(h)]
        running = None
        for i in reversed(range(count)):
            span = spans[i]
            grad = c_s[h, span, :].astype(F32) * gain * sq_s[span, :] - out_s[h, span, :] * mx_s[span, :]
            grad = grad.astype(BF16)
            g_s[h, span, :] = grad
            state = dot_tn(q_s[h, span, :] * first_s[span, :], grad)
            if i < count - 1:
                enter_s[1, h, i] = same(firsts[i + 1], lasts[i]) * running
                state = state + same(firsts[i + 1], firsts[i]) * running
            running = state
        own_s[1, h] = running

    @pl.loop(0, heads // pair)
    def _(step):
        group = [step * pair + i for i in range(pair)]
        for h in group:
            own_back(h)
        for h in group:
            send_own(1, h)

    def back_local(t):
        for i, span in enumerate(spans):
            scores = dot_nt(g_s[t, span, :], v_s[t, span, :]).astype(BF16) * mask_s[span, :]
            grad_q = dot_nn(scores, k_s[t, span, :])
            grad_q += dot_nt(g_s[t, span, :] * first_s[span, :], inc_s[t, i])
            dq_ref[span, lanes(t)] = grad_q.astype(BF16)
            turned = dot_nt(v_s[t, span, :], g_s[t, span, :]).astype(BF16) * maskt_s[span, :]
            part_s[t, span, :] = dot_nn(turned, q_s[t, span, :])
            dv_s[t, span, :] = dot_nn(st_s[t, span, :], g_s[t, span, :])

    def back_finish(h):
        returning = carry_s[1, h]
        for i, span in enumerate(spans):
            state = returning
            if i < count - 1:
                state = enter_s[1, h, i] + same(lasts[i], own_last) * returning
            state = state.astype(BF16)
            grad_k = part_s[h, span, :] + dot_nt(v_s[h, span, :] * last_s[span, :], state)
            dk_ref[span, lanes(h)] = grad_k.astype(BF16)
            grad_v = dv_s[h, span, :] + dot_nn(k_s[h, span, :] * last_s[span, :], state)
            dv_ref[span, lanes(h)] = grad_v.astype(BF16)

    run(1, back_local, back_finish)

    @pl.loop(0, heads)
    def _(h):
        for back in range(2):
            for i in range(len(parts)):
                state_copy(back, 0, h, i).wait_send()
                state_copy(back, 1, h, i).wait_send()

            @pl.when(has_down if back else has_up)
            def _():
                for i in range(len(parts)):
                    state_copy(back, 2, h, i).wait_send()

    meta_copy(0).wait_send()
    meta_copy(1).wait_send()

    @pl.when(has_up)
    def _():
        meta_copy(2).wait_send()

    @pl.when(has_down)
    def _():
        meta_copy(3).wait_send()

    for d in range(1, cores):
        stat_copy(d).wait_send()


def write_out(a_ref, b_ref, c_ref, a_out, b_out, c_out, sem):
    rows = a_ref.shape[0] // PIECES
    copies = []
    for i, (src, dst) in enumerate(((a_ref, a_out), (b_ref, b_out), (c_ref, c_out))):
        for j in range(PIECES):
            part = slice(j * rows, (j + 1) * rows)
            copies.append(pltpu.make_async_copy(src.at[part], dst.at[part], sem.at[i * PIECES + j]))
    for copy in copies:
        copy.start()
    for copy in copies:
        copy.wait()


def local(blocks, cores, query_vec, key_vec, value_vec, cotangent, norm_gain, doc_ids, lang_ids, loss_table):
    rows, cols = query_vec.shape
    heads = cols // HEAD_DIM
    count = rows // TILE
    state = (2, heads, HEAD_DIM, HEAD_DIM)
    per_head = (heads, rows, HEAD_DIM)
    any_spec = pl.BlockSpec(memory_space=pl.ANY)
    hbm_spec = pl.BlockSpec(memory_space=pltpu.HBM)
    vmem_spec = pl.BlockSpec(memory_space=pltpu.VMEM)
    operands = (
        loss_table,
        doc_ids.reshape(1, rows),
        lang_ids.reshape(1, rows),
        norm_gain.reshape(1, cols),
        query_vec,
        key_vec,
        value_vec,
        cotangent,
    )
    grads = pl.pallas_call(
        functools.partial(kernel, blocks, cores, HEADS * HEAD_DIM),
        out_shape=(pltpu.VMEM((rows, cols), BF16),) * 3,
        in_specs=[hbm_spec] * 8,
        out_specs=(vmem_spec,) * 3,
        scratch_shapes=[
            pltpu.SMEM(loss_table.shape, F32),
            pltpu.VMEM((1, rows), jnp.int32),
            pltpu.VMEM((1, rows), jnp.int32),
            pltpu.VMEM((1, cols), F32),
        ]
        + [pltpu.VMEM(per_head, BF16)] * 5
        + [pltpu.VMEM(per_head, F32)] * 3
        + [pltpu.VMEM((heads, rows, TILE), BF16)]
        + [pltpu.VMEM((rows, TILE), BF16)] * 2
        + [pltpu.VMEM(state, F32)] * 7
        + [
            pltpu.VMEM((heads, count) + state[2:], BF16),
            pltpu.VMEM((2, heads, count) + state[2:], F32),
            pltpu.VMEM((rows, HEAD_DIM), F32),
            pltpu.VMEM((rows, HEAD_DIM), BF16),
            pltpu.VMEM((rows, HEAD_DIM), BF16),
            pltpu.VMEM((rows, HEAD_DIM), F32),
            pltpu.VMEM((rows, HEAD_DIM), F32),
            pltpu.VMEM((8, rows), F32),
            pltpu.VMEM((max(cores - 1, 1), 8, rows), F32),
            pltpu.VMEM((7, 8, HEAD_DIM), F32),
            pltpu.SemaphoreType.DMA((4,)),
            pltpu.SemaphoreType.DMA((4, heads)),
            pltpu.SemaphoreType.DMA((2, 3, heads, HEAD_DIM // PART)),
            pltpu.SemaphoreType.DMA((2, 3, heads, HEAD_DIM // PART)),
            pltpu.SemaphoreType.DMA((4,)),
            pltpu.SemaphoreType.DMA((4,)),
            pltpu.SemaphoreType.DMA((max(cores - 1, 1),)),
            pltpu.SemaphoreType.DMA((max(cores - 1, 1),)),
        ],
        compiler_params=pltpu.CompilerParams(
            collective_id=0, has_side_effects=True, vmem_limit_bytes=VMEM_BYTES
        ),
    )(
        *(pltpu.with_memory_space_constraint(x, pltpu.HBM) for x in operands),
    )
    shape = jax.ShapeDtypeStruct((rows, cols), BF16)
    return pl.pallas_call(
        write_out,
        out_shape=(shape,) * 3,
        in_specs=[vmem_spec] * 3,
        out_specs=(any_spec,) * 3,
        scratch_shapes=[pltpu.SemaphoreType.DMA((3 * PIECES,))],
        compiler_params=pltpu.CompilerParams(vmem_limit_bytes=8 * 2**20),
    )(*(pltpu.with_memory_space_constraint(x, pltpu.VMEM) for x in grads))


def solution(mesh):
    sizes = dict(mesh.shape)
    in_specs = (
        P("seq", "head"),
        P("seq", "head"),
        P("seq", "head"),
        P("seq", "head"),
        P("head"),
        P("seq"),
        P("seq"),
        P(),
    )
    out_specs = (P("seq", "head"), P("seq", "head"), P("seq", "head"))
    body = functools.partial(local, sizes["seq"], sizes["head"])
    return jax.shard_map(body, mesh=mesh, in_specs=in_specs, out_specs=out_specs, check_vma=False)
```

```python
import functools

import jax
import jax.numpy as jnp
from jax import lax
from jax.experimental import pallas as pl
from jax.experimental.pallas import tpu as pltpu
from jax.sharding import PartitionSpec as P

HEAD_DIM = 128
HEADS = 16
EPSILON = 1e-06
TILE = 256
PART = 128
LAG_Y = 1
PIECES = 4
LAG_Z = 3
VMEM_BYTES = 44 * 2**20
MESH = pl.DeviceIdType.MESH
F32 = jnp.float32
BF16 = jnp.bfloat16


def dot_nn(a, b):
    return lax.dot_general(a, b, (((1,), (0,)), ((), ())), preferred_element_type=F32)


def dot_nt(a, b):
    return lax.dot_general(a, b, (((1,), (1,)), ((), ())), preferred_element_type=F32)


def dot_tn(a, b):
    return lax.dot_general(a, b, (((0,), (0,)), ((), ())), preferred_element_type=F32)


def same(a, b):
    return jnp.where(a == b, 1.0, 0.0)


def kernel(
    blocks, cores, norm_width,
    table_hbm, doc_hbm, lang_hbm, gain_hbm, q_hbm, k_hbm, v_hbm, c_hbm,
    dq_ref, dk_ref, dv_ref,
    table_ref, doc_ref, lang_ref, gain_ref,
    q_s, k_s, v_s, c_s, g_s, out_s, part_s, dv_s, st_s, mask_s, maskt_s,
    own_s, xin_s, pair_s, yin_s, send_s, zin_s, carry_s, inc_s, enter_s,
    col_s, first_s, last_s, sq_s, mx_s, stat_s, statin_s, meta_s,
    small_sem, in_sem, comm_send, comm_recv, meta_send, meta_recv, stat_send, stat_recv,
):
    heads, rows, _ = q_s.shape
    count = rows // TILE
    here = lax.axis_index("seq")
    core = lax.axis_index("head")
    bit_x = lax.rem(here, 2)
    bit_y = lax.rem(here // 2, 2)
    near = here + 1 - 2 * bit_x
    across = here + 2 - 4 * bit_y
    has_up = here + 4 < blocks
    has_down = here >= 4
    up = jnp.where(has_up, here + 4, here - 4)
    down = jnp.where(has_down, here - 4, here + 4)

    def load(which, h):
        src = (k_hbm, v_hbm, q_hbm, c_hbm)[which]
        dst = (k_s, v_s, q_s, c_s)[which]
        at = pl.ds(pl.multiple_of(h * HEAD_DIM, HEAD_DIM), HEAD_DIM)
        return pltpu.make_async_copy(src.at[:, at], dst.at[h], in_sem.at[which, h])

    def lanes(h):
        return pl.ds(pl.multiple_of(h * HEAD_DIM, HEAD_DIM), HEAD_DIM)

    small = [
        pltpu.make_async_copy(src, dst, small_sem.at[i])
        for i, (src, dst) in enumerate(
            ((doc_hbm, doc_ref), (lang_hbm, lang_ref), (gain_hbm, gain_ref), (table_hbm, table_ref))
        )
    ]
    for copy in small:
        copy.start()
    for group in ((0, 1), (2, 3)):
        for h in range(heads):
            for which in group:
                load(which, h).start()

    barrier = pltpu.get_barrier_semaphore()

    def greet(device):
        pl.semaphore_signal(barrier, inc=1, device_id=device, device_id_type=MESH)

    greet((near, core))
    greet((across, core))
    for d in range(1, cores):
        greet((here, lax.rem(core + d, cores)))

    @pl.when(has_up)
    def _():
        greet((up, core))

    @pl.when(has_down)
    def _():
        greet((down, core))

    def remote(src, dst, send_sem, recv_sem, device):
        return pltpu.make_async_remote_copy(
            src_ref=src, dst_ref=dst, send_sem=send_sem, recv_sem=recv_sem,
            device_id=device, device_id_type=MESH,
        )

    parts = [slice(i * PART, (i + 1) * PART) for i in range(HEAD_DIM // PART)]

    def state_copy(back, step, h, i):
        src = (own_s, pair_s, send_s)[step].at[back, h, parts[i]]
        dst = (xin_s, yin_s, zin_s)[step].at[back, h, parts[i]]
        target = (near, across, down if back else up)[step]
        return remote(
            src, dst, comm_send.at[back, step, h, i], comm_recv.at[back, step, h, i], (target, core)
        )

    def send_own(back, h):
        for i in range(len(parts)):
            state_copy(back, 0, h, i).start()

    def meta_copy(step):
        target = (near, across, up, down)[step]
        src = meta_s.at[(0, 2, 4, 4)[step]]
        dst = meta_s.at[(1, 3, 5, 6)[step]]
        return remote(src, dst, meta_send.at[step], meta_recv.at[step], (target, core))

    def stat_copy(d):
        return remote(
            stat_s, statin_s.at[d - 1], stat_send.at[d - 1], stat_recv.at[d - 1],
            (here, lax.rem(core + d, cores)),
        )

    def column(row):
        return jnp.transpose(jnp.broadcast_to(row, (HEAD_DIM, rows)))

    small[0].wait()
    doc_row = doc_ref[...].astype(F32)
    col_s[...] = column(doc_row)
    own_first = col_s[0:1, :]
    own_last = col_s[rows - 1 : rows, :]
    spans = [slice(i * TILE, (i + 1) * TILE) for i in range(count)]
    firsts = [col_s[i * TILE : i * TILE + 1, :] for i in range(count)]
    lasts = [col_s[(i + 1) * TILE - 1 : (i + 1) * TILE, :] for i in range(count)]
    for i, span in enumerate(spans):
        first_s[span, :] = same(col_s[span, :], firsts[i]).astype(BF16)
        last_s[span, :] = same(col_s[span, :], lasts[i]).astype(BF16)
    meta_s[0, 0:1, :] = own_first
    meta_s[0, 1:2, :] = own_last
    meta_s[0, 2:8, :] = jnp.zeros((6, HEAD_DIM), F32)

    total = 1 + 1 + (cores - 1) + has_up.astype(jnp.int32) + has_down.astype(jnp.int32)
    pl.semaphore_wait(barrier, total)
    meta_copy(0).start()

    def own_ahead(h):
        running = None
        for i, span in enumerate(spans):
            state = dot_tn(k_s[h, span, :] * last_s[span, :], v_s[h, span, :])
            if i > 0:
                enter_s[0, h, i] = same(lasts[i - 1], firsts[i]) * running
                state = state + same(lasts[i - 1], lasts[i]) * running
            running = state
        own_s[0, h] = running

    pair = 2 if heads % 2 == 0 else 1

    @pl.loop(0, heads // pair)
    def _(step):
        group = [step * pair + i for i in range(pair)]
        for h in group:
            load(0, h).wait()
            load(1, h).wait()
        for h in group:
            own_ahead(h)
        for h in group:
            send_own(0, h)

    ahead = lax.broadcasted_iota(jnp.int32, (TILE, HEAD_DIM), 0)
    lane = lax.broadcasted_iota(jnp.int32, (TILE, HEAD_DIM), 1)
    for i, span in enumerate(spans):
        col = col_s[span, :]
        for at in range(0, TILE, HEAD_DIM):
            start = i * TILE + at
            equal = col == doc_row[:, start : start + HEAD_DIM]
            mask_s[span, at : at + HEAD_DIM] = jnp.where(equal & (ahead >= lane + at), 1.0, 0.0).astype(BF16)
            maskt_s[span, at : at + HEAD_DIM] = jnp.where(equal & (ahead <= lane + at), 1.0, 0.0).astype(BF16)

    for copy in small[1:]:
        copy.wait()
    lang_row = lang_ref[...]
    weight_row = jnp.zeros((1, rows), F32)
    for i in range(table_ref.shape[0]):
        weight_row = jnp.where(lang_row == i, table_ref[i], weight_row)

    meta_copy(0).wait_recv()
    near_first = meta_s[1, 0:1, :]
    near_last = meta_s[1, 1:2, :]
    pair_first = jnp.where(bit_x == 0, own_first, near_first)
    pair_last = jnp.where(bit_x == 0, near_last, own_last)
    meta_s[2, 0:1, :] = pair_first
    meta_s[2, 1:2, :] = pair_last
    meta_s[2, 2:8, :] = jnp.zeros((6, HEAD_DIM), F32)
    meta_copy(1).start()
    sq_s[...] = jnp.zeros_like(sq_s)
    mx_s[...] = jnp.zeros_like(mx_s)
    meta_copy(1).wait_recv()
    other_first = meta_s[3, 0:1, :]
    other_last = meta_s[3, 1:2, :]
    group_first = jnp.where(bit_y == 0, pair_first, other_first)
    group_last = jnp.where(bit_y == 0, other_last, pair_last)
    meta_s[4, 0:1, :] = group_first
    meta_s[4, 1:2, :] = group_last
    meta_s[4, 2:8, :] = jnp.zeros((6, HEAD_DIM), F32)

    @pl.when(has_up)
    def _():
        meta_copy(2).start()

    @pl.when(has_down)
    def _():
        meta_copy(3).start()

    def factors(x, y, mine, target, theirs, other, group):
        x_on = x.astype(F32)
        y_on = y.astype(F32)
        equal = same(mine, theirs)
        pair = (jnp.where(x == 1, 1.0, equal), jnp.where(x == 1, equal, 1.0))
        take = (x_on * same(theirs, target), y_on * same(other, target))
        send = (same(mine, group), (1.0 - x_on) * same(theirs, group), 1.0 - y_on)
        return pair, take, send

    ahead_w = factors(bit_x, bit_y, own_last, own_first, near_last, other_last, group_last)
    back_w = factors(1 - bit_x, 1 - bit_y, own_first, own_last, near_first, other_first, group_first)

    def step_x(back, h):
        pair = (back_w if back else ahead_w)[0]
        for i, part in enumerate(parts):
            state_copy(back, 0, h, i).wait_recv()
            pair_s[back, h, part] = pair[0] * own_s[back, h, part] + pair[1] * xin_s[back, h, part]
            state_copy(back, 1, h, i).start()

    def step_y(back, h):
        take, send = (back_w if back else ahead_w)[1:]
        for i, part in enumerate(parts):
            state_copy(back, 1, h, i).wait_recv()
            near_state = xin_s[back, h, part]
            far_state = yin_s[back, h, part]
            send_s[back, h, part] = send[0] * own_s[back, h, part] + send[1] * near_state + send[2] * far_state

            @pl.when(has_down if back else has_up)
            def _():
                state_copy(back, 2, h, i).start()

            carry_s[back, h, part] = take[0] * near_state + take[1] * far_state

    def step_z(back, h):
        target = own_last if back else own_first

        @pl.when(has_up if back else has_down)
        def _():
            if back:
                end = meta_s[6, 0:1, :]
            else:
                end = meta_s[5, 1:2, :]
            for i in range(len(parts)):
                state_copy(back, 2, h, i).wait_recv()
            carry_s[back, h] += same(end, target) * zin_s[back, h]

    @pl.when(has_down)
    def _():
        meta_copy(2).wait_recv()

    @pl.when(has_up)
    def _():
        meta_copy(3).wait_recv()

    def ahead_local(t):
        for span in spans:
            scores = dot_nt(q_s[t, span, :], k_s[t, span, :]).astype(BF16) * mask_s[span, :]
            part_s[t, span, :] = dot_nn(scores, v_s[t, span, :])
            turned = dot_nt(k_s[t, span, :], q_s[t, span, :]).astype(BF16)
            st_s[t, span, :] = turned * maskt_s[span, :]

    def ahead_finish(h):
        incoming = carry_s[0, h]
        gain = gain_ref[:, lanes(h)]
        for i, span in enumerate(spans):
            state = incoming
            if i > 0:
                state = enter_s[0, h, i] + same(firsts[i], own_first) * incoming
            state = state.astype(BF16)
            inc_s[h, i] = state
            out = part_s[h, span, :] + dot_nn(q_s[h, span, :] * first_s[span, :], state)
            out_s[h, span, :] = out
            sq_s[span, :] += out * out
            mx_s[span, :] += c_s[h, span, :].astype(F32) * gain * out

    def run(back, local_part, finish):
        steps = heads // pair
        bounds = sorted({0, steps, LAG_Z, steps + LAG_Z})

        def group(step):
            return [step * pair + i for i in range(pair)]

        for begin, end in zip(bounds[:-1], bounds[1:]):
            with_local = end <= steps
            with_finish = begin >= LAG_Z

            @pl.loop(begin, end)
            def _(t):
                if with_local:
                    for h in group(t):
                        if not back:
                            load(2, h).wait()
                            load(3, h).wait()
                        step_x(back, h)

                @pl.when((t >= LAG_Y) & (t < steps + LAG_Y))
                def _():
                    for h in group(t - LAG_Y):
                        step_y(back, h)

                if with_finish:
                    for h in group(t - LAG_Z):
                        step_z(back, h)
                    for h in group(t - LAG_Z):
                        finish(h)
                if with_local:
                    for h in group(t):
                        local_part(h)

    run(0, ahead_local, ahead_finish)

    stat_s[0:1, :] = jnp.sum(jnp.transpose(sq_s[...]), axis=0, keepdims=True)
    stat_s[1:2, :] = jnp.sum(jnp.transpose(mx_s[...]), axis=0, keepdims=True)
    stat_s[2:8, :] = jnp.zeros((6, rows), F32)
    for d in range(1, cores):
        stat_copy(d).start()
    squares = stat_s[0:1, :]
    mixed = stat_s[1:2, :]
    for d in range(1, cores):
        stat_copy(d).wait_recv()
        squares = squares + statin_s[d - 1, 0:1, :]
        mixed = mixed + statin_s[d - 1, 1:2, :]
    inv_rms = lax.rsqrt(squares / norm_width + EPSILON)
    sq_s[...] = column(inv_rms * weight_row)
    mx_s[...] = column(inv_rms * inv_rms * inv_rms * (mixed * weight_row) / norm_width)

    def own_back(h):
        gain = gain_ref[:, lanes(h)]
        running = None
        for i in reversed(range(count)):
            span = spans[i]
            grad = c_s[h, span, :].astype(F32) * gain * sq_s[span, :] - out_s[h, span, :] * mx_s[span, :]
            grad = grad.astype(BF16)
            g_s[h, span, :] = grad
            state = dot_tn(q_s[h, span, :] * first_s[span, :], grad)
            if i < count - 1:
                enter_s[1, h, i] = same(firsts[i + 1], lasts[i]) * running
                state = state + same(firsts[i + 1], firsts[i]) * running
            running = state
        own_s[1, h] = running

    @pl.loop(0, heads // pair)
    def _(step):
        group = [step * pair + i for i in range(pair)]
        for h in group:
            own_back(h)
        for h in group:
            send_own(1, h)

    def back_local(t):
        for i, span in enumerate(spans):
            scores = dot_nt(g_s[t, span, :], v_s[t, span, :]).astype(BF16) * mask_s[span, :]
            grad_q = dot_nn(scores, k_s[t, span, :])
            grad_q += dot_nt(g_s[t, span, :] * first_s[span, :], inc_s[t, i])
            dq_ref[span, lanes(t)] = grad_q.astype(BF16)
            turned = dot_nt(v_s[t, span, :], g_s[t, span, :]).astype(BF16) * maskt_s[span, :]
            part_s[t, span, :] = dot_nn(turned, q_s[t, span, :])
            dv_s[t, span, :] = dot_nn(st_s[t, span, :], g_s[t, span, :])

    def back_finish(h):
        returning = carry_s[1, h]
        for i, span in enumerate(spans):
            state = returning
            if i < count - 1:
                state = enter_s[1, h, i] + same(lasts[i], own_last) * returning
            state = state.astype(BF16)
            grad_k = part_s[h, span, :] + dot_nt(v_s[h, span, :] * last_s[span, :], state)
            dk_ref[span, lanes(h)] = grad_k.astype(BF16)
            grad_v = dv_s[h, span, :] + dot_nn(k_s[h, span, :] * last_s[span, :], state)
            dv_ref[span, lanes(h)] = grad_v.astype(BF16)

    run(1, back_local, back_finish)

    @pl.loop(0, heads)
    def _(h):
        for back in range(2):
            for i in range(len(parts)):
                state_copy(back, 0, h, i).wait_send()
                state_copy(back, 1, h, i).wait_send()

            @pl.when(has_down if back else has_up)
            def _():
                for i in range(len(parts)):
                    state_copy(back, 2, h, i).wait_send()

    meta_copy(0).wait_send()
    meta_copy(1).wait_send()

    @pl.when(has_up)
    def _():
        meta_copy(2).wait_send()

    @pl.when(has_down)
    def _():
        meta_copy(3).wait_send()

    for d in range(1, cores):
        stat_copy(d).wait_send()


def write_out(a_ref, b_ref, c_ref, a_out, b_out, c_out, sem):
    rows = a_ref.shape[0] // PIECES
    copies = []
    for i, (src, dst) in enumerate(((a_ref, a_out), (b_ref, b_out), (c_ref, c_out))):
        for j in range(PIECES):
            part = slice(j * rows, (j + 1) * rows)
            copies.append(pltpu.make_async_copy(src.at[part], dst.at[part], sem.at[i * PIECES + j]))
    for copy in copies:
        copy.start()
    for copy in copies:
        copy.wait()


def local(blocks, cores, query_vec, key_vec, value_vec, cotangent, norm_gain, doc_ids, lang_ids, loss_table):
    rows, cols = query_vec.shape
    heads = cols // HEAD_DIM
    count = rows // TILE
    state = (2, heads, HEAD_DIM, HEAD_DIM)
    per_head = (heads, rows, HEAD_DIM)
    any_spec = pl.BlockSpec(memory_space=pl.ANY)
    hbm_spec = pl.BlockSpec(memory_space=pltpu.HBM)
    vmem_spec = pl.BlockSpec(memory_space=pltpu.VMEM)
    operands = (
        loss_table,
        doc_ids.reshape(1, rows),
        lang_ids.reshape(1, rows),
        norm_gain.reshape(1, cols),
        query_vec,
        key_vec,
        value_vec,
        cotangent,
    )
    grads = pl.pallas_call(
        functools.partial(kernel, blocks, cores, HEADS * HEAD_DIM),
        out_shape=(pltpu.VMEM((rows, cols), BF16),) * 3,
        in_specs=[hbm_spec] * 8,
        out_specs=(vmem_spec,) * 3,
        scratch_shapes=[
            pltpu.SMEM(loss_table.shape, F32),
            pltpu.VMEM((1, rows), jnp.int32),
            pltpu.VMEM((1, rows), jnp.int32),
            pltpu.VMEM((1, cols), F32),
        ]
        + [pltpu.VMEM(per_head, BF16)] * 5
        + [pltpu.VMEM(per_head, F32)] * 3
        + [pltpu.VMEM((heads, rows, TILE), BF16)]
        + [pltpu.VMEM((rows, TILE), BF16)] * 2
        + [pltpu.VMEM(state, F32)] * 7
        + [
            pltpu.VMEM((heads, count) + state[2:], BF16),
            pltpu.VMEM((2, heads, count) + state[2:], F32),
            pltpu.VMEM((rows, HEAD_DIM), F32),
            pltpu.VMEM((rows, HEAD_DIM), BF16),
            pltpu.VMEM((rows, HEAD_DIM), BF16),
            pltpu.VMEM((rows, HEAD_DIM), F32),
            pltpu.VMEM((rows, HEAD_DIM), F32),
            pltpu.VMEM((8, rows), F32),
            pltpu.VMEM((max(cores - 1, 1), 8, rows), F32),
            pltpu.VMEM((7, 8, HEAD_DIM), F32),
            pltpu.SemaphoreType.DMA((4,)),
            pltpu.SemaphoreType.DMA((4, heads)),
            pltpu.SemaphoreType.DMA((2, 3, heads, HEAD_DIM // PART)),
            pltpu.SemaphoreType.DMA((2, 3, heads, HEAD_DIM // PART)),
            pltpu.SemaphoreType.DMA((4,)),
            pltpu.SemaphoreType.DMA((4,)),
            pltpu.SemaphoreType.DMA((max(cores - 1, 1),)),
            pltpu.SemaphoreType.DMA((max(cores - 1, 1),)),
        ],
        compiler_params=pltpu.CompilerParams(
            collective_id=0, has_side_effects=True, vmem_limit_bytes=VMEM_BYTES
        ),
    )(
        *(pltpu.with_memory_space_constraint(x, pltpu.HBM) for x in operands),
    )
    shape = jax.ShapeDtypeStruct((rows, cols), BF16)
    return pl.pallas_call(
        write_out,
        out_shape=(shape,) * 3,
        in_specs=[vmem_spec] * 3,
        out_specs=(any_spec,) * 3,
        scratch_shapes=[pltpu.SemaphoreType.DMA((3 * PIECES,))],
        compiler_params=pltpu.CompilerParams(vmem_limit_bytes=8 * 2**20),
    )(*(pltpu.with_memory_space_constraint(x, pltpu.VMEM) for x in grads))


def solution(mesh):
    sizes = dict(mesh.shape)
    in_specs = (
        P("seq", "head"),
        P("seq", "head"),
        P("seq", "head"),
        P("seq", "head"),
        P("head"),
        P("seq"),
        P("seq"),
        P(),
    )
    out_specs = (P("seq", "head"), P("seq", "head"), P("seq", "head"))
    body = functools.partial(local, sizes["seq"], sizes["head"])
    return jax.shard_map(body, mesh=mesh, in_specs=in_specs, out_specs=out_specs, check_vma=False)
```
